128 devices in a mesh: gy: 16 (over y, z), gz: 8 (over x, core).
Axes of the slice: x: 4, y: 4, z: 4, core: 2. Of those that a mesh axis runs over, the one named last changes fastest.
Arguments:
- fields: float32 [12, 16, 1024, 1024], P(None, None, 'gy', 'gz'), may hold values from -6 to 6
- source_term: bfloat16 [12, 16, 1024, 1024], P(None, None, 'gy', 'gz'), may hold values from -15 to 15
- resistivity: float32 [1024], P('gz'), may hold values from 0.05 to 8000, as said below
Outputs:
- advanced: float32 [12, 16, 1024, 1024], P(None, None, 'gy', 'gz')
The draws below stay inside these ranges and needn't reach their ends.
Inputs may be any that keep to these rules, and one draw needn't show every extreme that they name: resistivity is positive.
All inputs are finite; a program needn't handle non-finite values.
Results may differ from the reference program's by a relative error of at most 0.005.
Values sent between devices are 32-bit elements; how exact they have to be, the bound alone decides.
No kernel may reach another device: no remote copies, remote signals or barrier semaphores. Data moves between devices by JAX's collectives and lax.ppermute only.
A program may use at most 128 MiB of HBM per device.

```python
import math
import jax
import jax.numpy as jnp
from jax import lax

COMPS = 12
NX = 16
STEPS = 1
NY = 1024
NZ = 1024


def draw_resistivity(key, part):
    key = jax.random.fold_in(key, 7)
    height = (jnp.arange(NZ, dtype=jnp.float32) + 0.5) / NZ - 0.5
    half_width = 0.5
    lowest = 0.5
    highest = 2.0
    shape_part = jnp.maximum(1.0 - (height / half_width) ** 2, 0.0)
    profile = 0.2 * jnp.exp(math.log(10000.0) * shape_part)
    rough_factor = jnp.exp(jax.random.uniform(key, (NZ,), jnp.float32, math.log(lowest), math.log(highest)))
    return profile * rough_factor


def levels(rng, extent, split, smallest, high):
    factor_of, own = 1.0, jax.random.fold_in(rng, 6)
    for dim, blocks in split:
        heights = jnp.exp(jax.random.uniform(jax.random.fold_in(own, dim), (blocks,), jnp.float32, smallest / len(split), high / len(split)))
        factor_of = factor_of * jnp.repeat(heights, extent[dim] // blocks).reshape([-1 if axis == dim else 1 for axis in range(len(extent))])
    return factor_of


def noise(own_key, dims, deviation, most, pieces=(), held_as=jnp.bfloat16):
    level = levels(own_key, dims, pieces, -0.22, 0.18) if pieces else 1.0
    values = jax.random.normal(own_key, dims, jnp.float32) * deviation * level
    return jnp.minimum(jnp.maximum(values, -most), most).astype(held_as)


def setup_inputs(seed: int = 0) -> dict:
    key_of = jax.random.split(jax.random.key(seed), 4)
    fields = noise(key_of[0], (COMPS, NX, NY, NZ), 1.0, 6.0, ((2, 16), (3, 8)), jnp.float32)
    source_term = noise(key_of[1], (COMPS, NX, NY, NZ), 3.0, 15.0, ((2, 16), (3, 8)))
    resistivity = draw_resistivity(jax.random.fold_in(key_of[3], 71), 0)
    return dict(fields=fields, source_term=source_term, resistivity=resistivity)


z_rate = 1.0
y_rate = 0.25

def cyclic_solve(sub_diag, middle, super_diag, right_side):
    length = middle.shape[-1]
    is_first = jnp.arange(length) == 0
    is_last = jnp.arange(length) == length - 1
    pivot = -middle[:, :1]
    corner_low = super_diag[:, -1:]
    corner_up = sub_diag[:, :1]
    adjusted = middle - jnp.where(is_first, pivot, 0.0) - jnp.where(is_last, corner_low * corner_up / pivot, 0.0)
    lower_band = jnp.where(is_first, 0.0, sub_diag)
    upper_band = jnp.where(is_last, 0.0, super_diag)
    primary = lax.linalg.tridiagonal_solve(lower_band, adjusted, upper_band, right_side)
    spike_vec = jnp.where(is_first, pivot, 0.0) + jnp.where(is_last, corner_low, 0.0)
    correction = lax.linalg.tridiagonal_solve(lower_band, adjusted, upper_band, spike_vec[:, :, None])
    ratio = corner_up[:, :, None] / pivot[:, :, None]
    weighting = (primary[:, :1, :] + ratio * primary[:, -1:, :]) / (1.0 + correction[:, :1, :] + ratio * correction[:, -1:, :])
    return primary - weighting * correction

def advance(tracer, forcing, resistivity):
    padded_eta = jnp.pad(resistivity, 1)
    faces = z_rate * 0.5 * (padded_eta[:-1] + padded_eta[1:])
    y_coef = y_rate * resistivity
    band_y = jnp.broadcast_to(-y_coef[:, None], (NZ, NY))
    middle_y = jnp.broadcast_to(1.0 + 2.0 * y_coef[:, None], (NZ, NY))
    zeros_one = jnp.zeros((1,), resistivity.dtype)
    sub_z = jnp.concatenate([zeros_one, -faces[1:NZ]])
    super_z = jnp.concatenate([-faces[1:NZ], zeros_one])
    middle_z = 1.0 + faces[:NZ] + faces[1:]
    for step_index in range(STEPS):
        padded = jnp.pad(tracer, ((0, 0), (0, 0), (1, 1)))
        explicit_z = faces[1:] * (padded[:, :, 2:] - tracer) - faces[:NZ] * (tracer - padded[:, :, :NZ])
        rhs_one = tracer + explicit_z + forcing
        line_data = jnp.transpose(rhs_one, (2, 1, 0))
        midway = jnp.transpose(cyclic_solve(band_y, middle_y, band_y, line_data), (2, 1, 0))
        explicit_y = y_coef * (jnp.roll(midway, 1, axis=1) + jnp.roll(midway, -1, axis=1) - 2.0 * midway)
        rhs_two = midway + explicit_y + forcing
        columns = rhs_two.reshape(NX * NY, NZ).T
        tracer = lax.linalg.tridiagonal_solve(sub_z, middle_z, super_z, columns).T.reshape(NX, NY, NZ)
    return tracer

def reference(fields, source_term, resistivity):

    def single(pair):
        return advance(pair[0], pair[1].astype(jnp.float32), resistivity)
    return lax.map(single, (fields, source_term))
```

```python
import jax
import jax.numpy as jnp
from jax import lax
from jax.experimental import pallas as pl
from jax.experimental.pallas import tpu as pltpu
from jax.sharding import PartitionSpec as P

f32 = jnp.float32
bf16 = jnp.bfloat16
z_rate = 1.0
y_rate = 0.25

LINES = 192
CY = 64
CZ = 128
GROUP = 8
PER = 32
STEPS = LINES // PER
PAIRS = PER // (2 * GROUP)
TILES = GROUP * CY // 8
NGY = 16
NGZ = 8
VMEM_LIMIT = 48 * 1024 * 1024


def lanes(shape=(8, CZ)):
    return lax.broadcasted_iota(jnp.int32, shape, len(shape) - 1)


def rows_of(shape=(8, CZ)):
    return lax.broadcasted_iota(jnp.int32, shape, 0)


def root_of(eta):
    k = y_rate * eta
    root = jnp.sqrt(1.0 + 4.0 * k)
    return 2.0 * k / (1.0 + 2.0 * k + root), 1.0 / root


def power_64(r):
    for _ in range(6):
        r = r * r
    return r


def split_3(x):
    high = x.astype(bf16)
    rest = x - high.astype(f32)
    mid = rest.astype(bf16)
    low = (rest - mid.astype(f32)).astype(bf16)
    return high, mid, low


def columns_kernel(u_ref, up_ref, down_ref):
    lane = lanes()
    odd = lane % 2 == 1

    def pair(p, _):
        packed = []
        for half in range(2):
            acc = jnp.zeros((8, CZ), f32)
            for k in range(TILES):
                line = (2 * p + half) * GROUP + k // 8
                tile = u_ref[line, pl.ds((k % 8) * 8, 8), :]
                if k:
                    tile = pltpu.roll(tile, 2 * k, 1)
                here = (lane == 2 * k) | (lane == (2 * k + CZ - 1) % CZ)
                acc = jnp.where(here, tile, acc)
            packed.append(acc)
        first, second = packed
        up_ref[p] = jnp.where(odd, first, pltpu.roll(second, 1, 1))
        down_ref[p] = jnp.where(odd, pltpu.roll(second, CZ - 1, 1), first)
        return 0

    lax.fori_loop(0, PAIRS, pair, 0)


def end_columns(u):
    return pl.pallas_call(
        columns_kernel,
        grid=(STEPS,),
        in_specs=[pl.BlockSpec((PER, CY, CZ), lambda i: (i, 0, 0))],
        out_specs=[pl.BlockSpec((PAIRS, 8, CZ), lambda i: (i, 0, 0))] * 2,
        out_shape=[jax.ShapeDtypeStruct((LINES // 16, 8, CZ), f32)] * 2,
        compiler_params=pltpu.CompilerParams(vmem_limit_bytes=VMEM_LIMIT),
        name="end_columns",
    )(u)


def sweep_kernel(rank_ref, u_ref, q_ref, low_ref, high_ref, eta_ref, m_ref, ends_ref, x_buf, f_buf):
    lane = lanes()
    even = lane % 2 == 0
    is_first = lane == 0
    is_last = lane == CZ - 1
    rank = rank_ref[0]
    eta_prev = jnp.broadcast_to(eta_ref[0:1, :], (8, CZ))
    eta = jnp.broadcast_to(eta_ref[1:2, :], (8, CZ))
    eta_next = jnp.broadcast_to(eta_ref[2:3, :], (8, CZ))
    eta_prev = jnp.where(rank > 0, eta_prev, 0.0)
    eta_next = jnp.where(rank < NGZ - 1, eta_next, 0.0)
    below = jnp.where(is_first, pltpu.roll(eta_prev, 1, 1), pltpu.roll(eta, 1, 1))
    above = jnp.where(is_last, pltpu.roll(eta_next, CZ - 1, 1), pltpu.roll(eta, CZ - 1, 1))
    face_low = z_rate * 0.5 * (below + eta)
    face_high = z_rate * 0.5 * (eta + above)
    decay, peak = root_of(eta)

    def pair(p, _):
        low, high = low_ref[p], high_ref[p]
        both = (
            jnp.where(even, pltpu.roll(low, 1, 1), pltpu.roll(high, CZ - 1, 1)),
            jnp.where(even, low, high),
        )
        for half in range(2):
            for k in range(TILES):
                line = (2 * p + half) * GROUP + k // 8
                at = pl.ds((k % 8) * 8, 8)
                here = u_ref[line, at, :]
                halo = both[half] if k == 0 else pltpu.roll(both[half], (CZ - 2 * k) % CZ, 1)
                under = jnp.where(is_first, halo, pltpu.roll(here, 1, 1))
                over = jnp.where(is_last, halo, pltpu.roll(here, CZ - 1, 1))
                q = q_ref[line, at, :].astype(f32)
                explicit = face_high * (over - here) - face_low * (here - under)
                x_buf[pl.ds(line * CY + (k % 8) * 8, 8), :] = here + explicit + q
        return 0

    lax.fori_loop(0, PAIRS, pair, 0)

    groups = PER // GROUP

    def at(g, y):
        return pl.ds(g * GROUP * CY + y, GROUP, stride=CY)

    total = [jnp.zeros((8, CZ), f32) for _ in range(groups)]
    for y in range(CY):
        for g in range(groups):
            total[g] = total[g] * decay + x_buf[at(g, y), :]
            f_buf[at(g, y), :] = total[g]
    for g in range(groups):
        ends_ref[0, pl.ds(g * GROUP, GROUP), :] = total[g]
    total = [jnp.zeros((8, CZ), f32) for _ in range(groups)]
    for y in reversed(range(CY)):
        for g in range(groups):
            kept = total[g] * decay
            total[g] = kept + x_buf[at(g, y), :]
            f_buf[at(g, y), :] = peak * (f_buf[at(g, y), :] + kept)
    for g in range(groups):
        ends_ref[1, pl.ds(g * GROUP, GROUP), :] = total[g]

    def copy(line, _):
        m_ref[line] = f_buf[pl.ds(pl.multiple_of(line * CY, CY), CY), :]
        return 0

    lax.fori_loop(0, PER, copy, 0)


def sweeps(ranks, u, q, low, high, etas):
    block = pl.BlockSpec((PER, CY, CZ), lambda i: (i, 0, 0))
    halo = pl.BlockSpec((PAIRS, 8, CZ), lambda i: (i, 0, 0))
    return pl.pallas_call(
        sweep_kernel,
        grid=(STEPS,),
        in_specs=[
            pl.BlockSpec(memory_space=pltpu.SMEM),
            block,
            block,
            halo,
            halo,
            pl.BlockSpec((8, CZ), lambda i: (0, 0)),
        ],
        out_specs=[block, pl.BlockSpec((2, PER, CZ), lambda i: (0, i, 0))],
        out_shape=[
            jax.ShapeDtypeStruct((LINES, CY, CZ), f32),
            jax.ShapeDtypeStruct((2, LINES, CZ), f32),
        ],
        scratch_shapes=[pltpu.VMEM((PER * CY, CZ), f32)] * 2,
        compiler_params=pltpu.CompilerParams(vmem_limit_bytes=VMEM_LIMIT),
        name="y_sweeps",
    )(ranks, u, q, low, high, etas)


def ring_kernel(rank_ref, ends_ref, eta_ref, out_ref):
    rows = 2 * LINES // NGY
    upward = rank_ref[1] < NGY // 2
    decay, _ = root_of(jnp.broadcast_to(eta_ref[1:2, :], (8, CZ)))
    whole = power_64(decay)
    turn = whole
    for _ in range(4):
        turn = turn * turn
    closing = 1.0 / (1.0 - turn)
    for part in range(rows // 8):

        def at(node):
            return pl.ds(node * rows + part * 8, 8)

        up = jnp.zeros((8, CZ), f32)
        down = jnp.zeros((8, CZ), f32)
        for node in range(NGY):
            up = up * whole + ends_ref[at(node), :]
            down = down * whole + ends_ref[at(NGY - 1 - node), :]
        up = up * closing
        down = down * closing
        ups, downs = [], [None] * NGY
        for node in range(NGY):
            ups.append(up)
            up = up * whole + ends_ref[at(node), :]
            downs[NGY - 1 - node] = down
            down = down * whole + ends_ref[at(NGY - 1 - node), :]
        for node in range(NGY):
            out_ref[at(node), :] = jnp.where(upward, ups[node], downs[node])


def ring_scan(ranks, ends, etas):
    return pl.pallas_call(
        ring_kernel,
        in_specs=[
            pl.BlockSpec(memory_space=pltpu.SMEM),
            pl.BlockSpec(memory_space=pltpu.VMEM),
            pl.BlockSpec(memory_space=pltpu.VMEM),
        ],
        out_specs=pl.BlockSpec(memory_space=pltpu.VMEM),
        out_shape=jax.ShapeDtypeStruct(ends.shape, f32),
        name="ring_scan",
    )(ranks, ends, etas)


def coefficient_kernel(rank_ref, eta_ref, table_ref, weight_ref, vector_ref, share_ref):
    rank = rank_ref[0]
    lane, row = lanes(), rows_of()
    eta = pltpu.roll(eta_ref[...], lax.rem(rank + 5, 8), 0)

    def before(x, fill):
        y = pltpu.roll(x, 1, 1)
        return jnp.where(lane == 0, jnp.where(row == 0, fill, pltpu.roll(y, 1, 0)), y)

    def after(x, fill):
        y = pltpu.roll(x, CZ - 1, 1)
        edge = jnp.where(row == NGZ - 1, fill, pltpu.roll(y, NGZ - 1, 0))
        return jnp.where(lane == CZ - 1, edge, y)

    def last_of(x, end):
        return jnp.broadcast_to(x[:, end : end + 1], (8, CZ))

    face_low = z_rate * 0.5 * (before(eta, 0.0) + eta)
    face_high = z_rate * 0.5 * (eta + after(eta, 0.0))

    def pivots(face, up):
        scale = 1.0 / (1.0 + face)
        a = jnp.ones((8, CZ), f32)
        b = face * scale
        c = scale
        d = b
        step = 1
        while step < CZ:
            shift = step if up else CZ - step
            inside = lane >= step if up else lane < CZ - step
            pa, pb, pc, pd = (pltpu.roll(x, shift, 1) for x in (a, b, c, d))
            na, nb = a * pa + b * pc, a * pb + b * pd
            nc, nd = c * pa + d * pc, c * pb + d * pd
            a, b = jnp.where(inside, na, a), jnp.where(inside, nb, b)
            c, d = jnp.where(inside, nc, c), jnp.where(inside, nd, d)
            step *= 2
        end = CZ - 1 if up else 0
        ta, tb, tc, td = (last_of(x, end) for x in (a, b, c, d))
        edge = row == (0 if up else NGZ - 1)
        va, vc = jnp.ones((8, CZ), f32), jnp.zeros((8, CZ), f32)
        for _ in range(NGZ - 1):
            na, nc = ta * va + tb * vc, tc * va + td * vc
            size = 1.0 / (na + nc)
            shift = 1 if up else NGZ - 1
            va = jnp.where(edge, 1.0, pltpu.roll(na * size, shift, 0))
            vc = jnp.where(edge, 0.0, pltpu.roll(nc * size, shift, 0))
        return (a * va + b * vc) / (c * va + d * vc)

    delta_up = pivots(face_low, True)
    delta_down = pivots(face_high, False)
    inverse = 1.0 / (delta_up + delta_down - 1.0)
    first_cell = (lane == 0) & (row == 0)
    last_cell = (lane == CZ - 1) & (row == NGZ - 1)
    link_up = jnp.where(first_cell, 0.0, face_low / (face_low + before(delta_up, 1.0)))
    link_down = jnp.where(last_cell, 0.0, face_high / (face_high + after(delta_down, 1.0)))

    def running(x, up):
        step = 1
        while step < CZ:
            moved = pltpu.roll(x, step if up else CZ - step, 1)
            x = jnp.where(lane >= step if up else lane < CZ - step, x * moved, x)
            step *= 2
        return x

    product_up, product_down = running(link_up, True), running(link_down, False)
    across_up, across_down = last_of(product_up, CZ - 1), last_of(product_down, 0)
    share_up = jnp.zeros((8, CZ), f32)
    share_down = jnp.zeros((8, CZ), f32)
    for _ in range(NGZ - 1):
        moved = pltpu.roll(across_up * share_up, NGZ - 1, 0)
        share_up = jnp.where(row == rank - 1, 1.0, jnp.where(row < rank - 1, moved, 0.0))
        moved = pltpu.roll(across_down * share_down, 1, 0)
        share_down = jnp.where(row == rank + 1, 1.0, jnp.where(row > rank + 1, moved, 0.0))
    back = lax.rem(NGZ - rank, NGZ)
    share_ref[0] = pltpu.roll(share_up, back, 0)
    share_ref[1] = pltpu.roll(share_down, back, 0)

    def own(x):
        return jnp.sum(jnp.where(row == rank, x, 0.0), axis=0, keepdims=True)

    scale = own(inverse)
    vector_ref[0:1, :] = own(product_up) * scale
    vector_ref[1:2, :] = own(product_down) * scale

    square = (CZ, CZ)
    lane_sq, row_sq = lanes(square), rows_of(square)
    identity = jnp.where(lane_sq == row_sq, 1.0, 0.0).astype(f32)

    def triangle(link, up):
        link = jnp.where(lanes((1, CZ)) == (0 if up else CZ - 1), 0.0, link)
        link = jnp.broadcast_to(link, (8, CZ))
        out = identity
        step = 1
        while step < CZ:
            shift = step if up else CZ - step
            out = out + jnp.broadcast_to(link[0:1, :], square) * pltpu.roll(out, shift, 1)
            link = link * pltpu.roll(link, shift, 1)
            step *= 2
        return out

    lower, upper = triangle(own(link_up), True), triangle(own(link_down), False)
    green = 2.0 * (lower + upper - identity) * jnp.broadcast_to(scale, square)
    ends = 2.0 * jnp.where(
        lane_sq < CZ // 2,
        jnp.broadcast_to(lower[:, CZ - 1 : CZ], square),
        jnp.broadcast_to(upper[:, 0:1], square),
    )
    for half, matrix in enumerate((green, ends)):
        high, mid, low = split_3(matrix)
        columns = pl.ds(half * CZ, CZ)
        for place, part in enumerate((high, high, mid, mid, high, low)):
            weight_ref[pl.ds(place * CZ, CZ), columns] = part

    decay, peak = root_of(own(eta))
    tall = (CY, CZ)
    y = rows_of(tall)
    powers_up = jnp.broadcast_to(peak * decay, tall)
    powers_down = powers_up
    factor = decay
    for bit in range(6):
        wide = jnp.broadcast_to(factor, tall)
        powers_up = jnp.where((y >> bit) & 1 == 1, powers_up * wide, powers_up)
        powers_down = jnp.where(((CY - 1 - y) >> bit) & 1 == 1, powers_down * wide, powers_down)
        factor = factor * factor
    table_ref[0] = powers_up
    table_ref[1] = powers_down


def coefficients(ranks, etas):
    vmem = pl.BlockSpec(memory_space=pltpu.VMEM)
    return pl.pallas_call(
        coefficient_kernel,
        in_specs=[pl.BlockSpec(memory_space=pltpu.SMEM), vmem],
        out_specs=[vmem] * 4,
        out_shape=[
            jax.ShapeDtypeStruct((2, CY, CZ), f32),
            jax.ShapeDtypeStruct((6 * CZ, 2 * CZ), bf16),
            jax.ShapeDtypeStruct((8, CZ), f32),
            jax.ShapeDtypeStruct((2, NGZ, CZ), f32),
        ],
        name="z_coefficients",
    )(ranks, etas)


def solve_kernel(rank_ref, m_ref, u_ref, carry_ref, table_ref, weight_ref, out_ref, *rest):
    message_refs, left = rest[: NGZ - 1], rest[NGZ - 1]
    rank = rank_ref[0]
    lane = lanes()

    def pair(p, _):
        packed = []
        for half in range(2):
            for c in range(GROUP):
                line = (2 * p + half) * GROUP + c
                tall = (CY, CZ)
                carry_up = jnp.broadcast_to(carry_ref[0, pl.ds(line, 1), :], tall)
                carry_down = jnp.broadcast_to(carry_ref[1, pl.ds(line, 1), :], tall)
                change = m_ref[line] - u_ref[line]
                change = change + table_ref[0] * carry_up + table_ref[1] * carry_down
                high, mid, low = split_3(change)
                at = pl.ds(c * CY, CY)
                left[at, 0:CZ] = high
                left[at, CZ : 2 * CZ] = mid
                left[at, 2 * CZ : 3 * CZ] = low
                left[at, 3 * CZ : 4 * CZ] = high
            near = left[:, : 2 * CZ]
            result = jnp.dot(near, weight_ref[: 2 * CZ], preferred_element_type=f32)
            result += jnp.dot(near, weight_ref[2 * CZ : 4 * CZ], preferred_element_type=f32)
            result += jnp.dot(
                left[:, 2 * CZ :], weight_ref[4 * CZ :], preferred_element_type=f32
            )
            for c in range(GROUP):
                line = (2 * p + half) * GROUP + c
                out_ref[line] = u_ref[line] + result[c * CY : (c + 1) * CY, :CZ]
            acc = jnp.zeros((8, CZ), f32)
            for k in range(TILES):
                acc = jnp.where(lane % 64 == k, result[8 * k : 8 * k + 8, CZ:], acc)
            packed.append(acc)
        first, second = packed
        up = jnp.where(lane < 64, first, pltpu.roll(second, 64, 1))
        down = jnp.where(lane < 64, pltpu.roll(first, 64, 1), second)
        for k in range(1, NGZ):
            message_refs[k - 1][p] = jnp.where(rank >= k, down, up)
        return 0

    lax.fori_loop(0, PAIRS, pair, 0)


def local_solve(ranks, m, u, carries, table, weight):
    block = pl.BlockSpec((PER, CY, CZ), lambda i: (i, 0, 0))
    message = pl.BlockSpec((PAIRS, 8, CZ), lambda i: (i, 0, 0))
    return pl.pallas_call(
        solve_kernel,
        grid=(STEPS,),
        in_specs=[
            pl.BlockSpec(memory_space=pltpu.SMEM),
            block,
            block,
            pl.BlockSpec((2, PER, CZ), lambda i: (0, i, 0)),
            pl.BlockSpec((2, CY, CZ), lambda i: (0, 0, 0)),
            pl.BlockSpec((6 * CZ, 2 * CZ), lambda i: (0, 0)),
        ],
        out_specs=[block] + [message] * (NGZ - 1),
        out_shape=[jax.ShapeDtypeStruct((LINES, CY, CZ), f32)]
        + [jax.ShapeDtypeStruct((LINES // 16, 8, CZ), f32)] * (NGZ - 1),
        scratch_shapes=[pltpu.VMEM((GROUP * CY, 4 * CZ), bf16)],
        compiler_params=pltpu.CompilerParams(vmem_limit_bytes=VMEM_LIMIT),
        name="z_local_solve",
    )(ranks, m, u, carries, table, weight)


def finish_kernel(y_ref, vector_ref, share_ref, *rest):
    got, out_ref = rest[: NGZ - 1], rest[NGZ - 1]
    lane = lanes()
    left = jnp.broadcast_to(vector_ref[0:1, :], (8, CZ))
    right = jnp.broadcast_to(vector_ref[1:2, :], (8, CZ))

    def pair(p, _):
        up = jnp.zeros((8, CZ), f32)
        down = jnp.zeros((8, CZ), f32)
        for k in range(1, NGZ):
            value = got[k - 1][p]
            up += jnp.broadcast_to(share_ref[0, k : k + 1, :], (8, CZ)) * value
            down += jnp.broadcast_to(share_ref[1, k : k + 1, :], (8, CZ)) * value
        both = (
            jnp.where(lane < 64, up, pltpu.roll(down, 64, 1)),
            jnp.where(lane < 64, pltpu.roll(up, 64, 1), down),
        )
        for half in range(2):
            for k in range(TILES):
                line = (2 * p + half) * GROUP + k // 8
                at = pl.ds((k % 8) * 8, 8)
                low = jnp.broadcast_to(both[half][:, k : k + 1], (8, CZ))
                high = jnp.broadcast_to(both[half][:, 64 + k : 65 + k], (8, CZ))
                out_ref[line, at, :] = y_ref[line, at, :] + low * left + high * right
        return 0

    lax.fori_loop(0, PAIRS, pair, 0)


def finish(y, vector, share, got):
    block = pl.BlockSpec((PER, CY, CZ), lambda i: (i, 0, 0))
    message = pl.BlockSpec((PAIRS, 8, CZ), lambda i: (i, 0, 0))
    return pl.pallas_call(
        finish_kernel,
        grid=(STEPS,),
        in_specs=[
            block,
            pl.BlockSpec((8, CZ), lambda i: (0, 0)),
            pl.BlockSpec((2, NGZ, CZ), lambda i: (0, 0, 0)),
        ]
        + [message] * (NGZ - 1),
        out_specs=block,
        out_shape=jax.ShapeDtypeStruct((LINES, CY, CZ), f32),
        compiler_params=pltpu.CompilerParams(vmem_limit_bytes=VMEM_LIMIT),
        name="z_carries",
    )(y, vector, share, *got)


def shifted(x, axis, by, wrap=True):
    n = lax.axis_size(axis)
    pairs = [(i, (i + by) % n) for i in range(n) if wrap or 0 <= i + by < n]
    return lax.ppermute(x, axis, pairs)


def body(fields, source_term, resistivity):
    u = fields.reshape(LINES, CY, CZ)
    q = source_term.reshape(LINES, CY, CZ)
    ranks = jnp.stack([lax.axis_index("gz"), lax.axis_index("gy")]).astype(jnp.int32)
    own = resistivity.reshape(1, CZ)
    prev_eta, next_eta = shifted(own, "gz", 1), shifted(own, "gz", -1)
    near = jnp.concatenate([prev_eta, own, next_eta, jnp.zeros((5, CZ), f32)], axis=0)
    up, down = end_columns(u)
    low = shifted(up, "gz", 1, wrap=False)
    high = shifted(down, "gz", -1, wrap=False)
    far_low, far_high = shifted(near, "gz", 3), shifted(near, "gz", -3)
    all_eta = jnp.concatenate([far_low[1:3], near[:3], far_high[:3]], axis=0)
    table, weight, vector, share = coefficients(ranks, all_eta)
    m, ends = sweeps(ranks, u, q, low, high, near)
    nodes = lax.all_to_all(ends.reshape(2 * LINES, CZ), "gy", 0, 0, tiled=True)
    nodes = ring_scan(ranks, nodes, near)
    carries = lax.all_to_all(nodes, "gy", 0, 0, tiled=True).reshape(2, LINES, CZ)
    y, *messages = local_solve(ranks, m, u, carries, table, weight)
    got = [shifted(x, "gz", -k) for k, x in enumerate(messages, start=1)]
    return finish(y, vector, share, got).reshape(fields.shape)


def solution(mesh):
    return jax.shard_map(
        body,
        mesh=mesh,
        in_specs=(P(None, None, "gy", "gz"), P(None, None, "gy", "gz"), P("gz")),
        out_specs=P(None, None, "gy", "gz"),
        check_vma=False,
    )
```

```python
import jax
import jax.numpy as jnp
from jax import lax
from jax.experimental import pallas as pl
from jax.experimental.pallas import tpu as pltpu
from jax.sharding import PartitionSpec as P

f32 = jnp.float32
bf16 = jnp.bfloat16
z_rate = 1.0
y_rate = 0.25

LINES = 192
CY = 64
CZ = 128
GROUP = 8
PER = 32
STEPS = LINES // PER
SLOTS = 2
AHEAD = 3
PITCH = 65
NGY = 16
NGZ = 8


def lanes(shape=(8, CZ)):
    return lax.broadcasted_iota(jnp.int32, shape, len(shape) - 1)


def rows_of(shape=(8, CZ)):
    return lax.broadcasted_iota(jnp.int32, shape, 0)


def root_of(eta):
    k = y_rate * eta
    root = jnp.sqrt(1.0 + 4.0 * k)
    return 2.0 * k / (1.0 + 2.0 * k + root), 1.0 / root


def power_64(r):
    for _ in range(6):
        r = r * r
    return r


def split(x):
    high = x.astype(bf16)
    return high, (x - high.astype(f32)).astype(bf16)


def chunk(ref, step):
    return ref.at[pl.ds(step * PER, PER)]


def kernel_call(kernel, out_shape, out_specs, in_specs, scratch=(), name=None, us=1):
    return pl.pallas_call(
        kernel,
        in_specs=in_specs,
        out_specs=out_specs,
        out_shape=out_shape,
        scratch_shapes=list(scratch),
        compiler_params=pltpu.CompilerParams(vmem_limit_bytes=60 * 1024 * 1024),
        cost_estimate=pl.CostEstimate(flops=0, bytes_accessed=us * 3_000_000, transcendentals=0),
        name=name,
    )


def pipeline(fetches, stores, work, prepare=None):
    for i in range(AHEAD):
        for copy in fetches(i):
            copy.start()
    if prepare:
        prepare()

    def step(i, _):
        @pl.when(i + AHEAD < STEPS)
        def _():
            for copy in fetches(i + AHEAD):
                copy.start()

        for copy in fetches(i):
            copy.wait()
        work(i)
        for copy in stores(i):
            copy.start()
        return 0

    lax.fori_loop(0, STEPS, step, 0)

    def drain(i, _):
        for copy in stores(i):
            copy.wait()
        return 0

    lax.fori_loop(0, STEPS, drain, 0)


def pitched(ref, step):
    return ref.at[pl.ds(step * PER * PITCH, PER * PITCH)]


def no_copies(i):
    return ()


def unit_mask(tall):
    return (lanes(tall) & 63) == rows_of(tall)


VMEM = pl.BlockSpec(memory_space=pltpu.VMEM)
SMEM = pl.BlockSpec(memory_space=pltpu.SMEM)
HBM = pl.BlockSpec(memory_space=pltpu.HBM)
CUBE = jax.ShapeDtypeStruct((LINES, CY, CZ), f32)
FLAT = jax.ShapeDtypeStruct((LINES, CZ), f32)
PITCHED = (LINES * PITCH, CZ)
ROWS = LINES // 2


def sweep_kernel(
    u_hbm, q_hbm, eta_ref, m_hbm, ends_ref, columns_ref, u_ref, q_ref, m_ref, x_buf, f_buf, sems
):
    lane = lanes()
    place = ((lane + 1) >> 1) & 63

    def fetches(i):
        return (
            pltpu.make_async_copy(chunk(u_hbm, i), chunk(u_ref, i), sems.at[0, i]),
            pltpu.make_async_copy(chunk(q_hbm, i), chunk(q_ref, i), sems.at[1, i]),
        )

    def stores(i):
        return (pltpu.make_async_copy(pitched(m_ref, i), pitched(m_hbm, i), sems.at[2, i]),)

    eta = jnp.broadcast_to(eta_ref[...], (8, CZ))
    columns_ref[pl.ds(LINES, 8), :] = eta
    face_low = jnp.where(lane == 0, 0.0, z_rate * 0.5 * (pltpu.roll(eta, 1, 1) + eta))
    face_high = jnp.where(lane == CZ - 1, 0.0, z_rate * 0.5 * (eta + pltpu.roll(eta, CZ - 1, 1)))
    decay, peak = root_of(eta)
    groups = PER // GROUP

    def work(i):
        def rows(g):
            return pl.ds(pl.multiple_of(i * PER + g * GROUP, 8), GROUP)

        def right_side(g, _):
            acc = jnp.zeros((8, CZ), f32)
            for k in range(8 * GROUP):
                c, at = g * GROUP + k // 8, pl.ds((k % 8) * 8, 8)
                here = u_ref[i * PER + c, at, :]
                under = pltpu.roll(here, 1, 1)
                over = pltpu.roll(here, CZ - 1, 1)
                acc = jnp.where(place == k, pltpu.roll(here, 2 * k, 1) if k else here, acc)
                q = q_ref[i * PER + c, at, :].astype(f32)
                explicit = face_high * (over - here) - face_low * (here - under)
                x_buf[pl.ds(c * PITCH + (k % 8) * 8, 8), :] = here + explicit + q
            columns_ref[rows(g), :] = acc
            return 0

        lax.fori_loop(0, groups, right_side, 0)

        def at(g, y):
            return pl.ds(g * GROUP * PITCH + y, GROUP, stride=PITCH)

        def out(g, y):
            return pl.ds((i * PER + g * GROUP) * PITCH + y, GROUP, stride=PITCH)

        total = [jnp.zeros((8, CZ), f32) for _ in range(groups)]
        for y in range(CY):
            for g in range(groups):
                total[g] = total[g] * decay + x_buf[at(g, y), :]
                f_buf[at(g, y), :] = total[g]
        for g in range(groups):
            ends_ref[0, rows(g), :] = total[g]
        total = [jnp.zeros((8, CZ), f32) for _ in range(groups)]
        for y in reversed(range(CY)):
            for g in range(groups):
                kept = total[g] * decay
                total[g] = kept + x_buf[at(g, y), :]
                m_ref[out(g, y), :] = peak * (f_buf[at(g, y), :] + kept)
        for g in range(groups):
            ends_ref[1, rows(g), :] = total[g]

    pipeline(fetches, stores, work)


def sweeps(u, q, own):
    return kernel_call(
        sweep_kernel,
        [
            jax.ShapeDtypeStruct(PITCHED, f32),
            jax.ShapeDtypeStruct((2, LINES, CZ), f32),
            jax.ShapeDtypeStruct((LINES + 8, CZ), f32),
        ],
        [HBM, VMEM, VMEM],
        [HBM, HBM, VMEM],
        [
            pltpu.VMEM((LINES, CY, CZ), f32),
            pltpu.VMEM((LINES, CY, CZ), bf16),
            pltpu.VMEM(PITCHED, f32),
            pltpu.VMEM((PER * PITCH, CZ), f32),
            pltpu.VMEM((PER * PITCH, CZ), f32),
            pltpu.SemaphoreType.DMA((3, STEPS)),
        ],
        name="y_sweeps",
        us=12,
    )(u, q, own)


def raised(base, exponent, bits=6):
    out = jnp.ones_like(base)
    for bit in range(bits):
        out = jnp.where((exponent >> bit) & 1 == 1, out * base, out)
        base = base * base
    return out


def exact_dot(a, b):
    return jnp.dot(a, b, preferred_element_type=f32, precision=lax.Precision.HIGHEST)


def flux_place(l):
    return 8 * ((l >> 1) & 7) + (l >> 4), l & 1


def turned(x):
    lane, row = lanes(x.shape), rows_of(x.shape)
    for bit in range(3):
        rows, columns = 1 << bit, 16 << bit
        in_row, in_lane = (row >> bit) & 1, (lane >> (4 + bit)) & 1
        count = x.shape[0]
        forth = pltpu.roll(pltpu.roll(x, count - rows, 0), columns, 1)
        back = pltpu.roll(pltpu.roll(x, rows, 0), CZ - columns, 1)
        x = jnp.where(in_row == in_lane, x, jnp.where(in_row == 0, forth, back))
    return x


def repair_kernel(rank_ref, ends_ref, columns_ref, low_ref, high_ref, out_ref, flux_ref, near_ref):
    rank = rank_ref[0]
    square = (CZ, CZ)
    lane = lanes(square)
    inner_low, inner_high = rank > 0, rank < NGZ - 1
    own_eta, low_eta, high_eta = (
        ref[pl.ds(LINES, 8), :] for ref in (columns_ref, low_ref, high_ref)
    )
    row = rows_of()
    near_ref[...] = jnp.where(row == 0, low_eta, jnp.where(row == 1, own_eta, high_eta))
    own = own_eta[:1]
    low_eta = jnp.where(inner_low, low_eta[:1], 0.0)[:, CZ - 1 :]
    high_eta = jnp.where(inner_high, high_eta[:1], 0.0)[:, :1]
    face_low = jnp.broadcast_to(z_rate * 0.5 * (low_eta + own[:, :1]), (1, CZ))
    face_high = jnp.broadcast_to(z_rate * 0.5 * (own[:, CZ - 1 :] + high_eta), (1, CZ))
    even = lanes((LINES, CZ)) & 1 == 0
    low, high, columns = (ref[pl.ds(0, LINES), :] for ref in (low_ref, high_ref, columns_ref))
    outer = jnp.where(
        even,
        jnp.where(inner_low, pltpu.roll(low, 1, 1), 0.0),
        jnp.where(inner_high, pltpu.roll(high, 1, 1), 0.0),
    )
    inner = jnp.where(even, columns, pltpu.roll(columns, 2, 1))
    face = jnp.where(lanes((1, CZ)) & 1 == 0, face_low, face_high)
    flux = turned(jnp.broadcast_to(face, (LINES, CZ)) * (outer - inner))
    flux_ref[...] = flux
    decay, _ = root_of(own)
    y, side = flux_place(rows_of(square))
    base = jnp.where(
        side == 0,
        jnp.broadcast_to(decay[:, :1], square),
        jnp.broadcast_to(decay[:, CZ - 1 :], square),
    )
    place = lane == jnp.where(side == 0, 0, CZ - 1)
    out_ref[0] = ends_ref[0] + exact_dot(flux, jnp.where(place, raised(base, 63 - y), 0.0))
    out_ref[1] = ends_ref[1] + exact_dot(flux, jnp.where(place, raised(base, y), 0.0))


def repair(ranks, ends, columns, low, high):
    shapes = [
        jax.ShapeDtypeStruct((2, LINES, CZ), f32),
        FLAT,
        jax.ShapeDtypeStruct((NGZ, CZ), f32),
    ]
    call = kernel_call(repair_kernel, shapes, [VMEM] * 3, [SMEM] + [VMEM] * 4, name="repair")
    return call(ranks, ends, columns, low, high)


def ring_kernel(rank_ref, ends_ref, eta_ref, out_ref):
    rows = 2 * LINES // NGY
    upward = rank_ref[1] < NGY // 2
    decay, _ = root_of(jnp.broadcast_to(eta_ref[...], (8, CZ)))
    whole = power_64(decay)
    turn = whole
    for _ in range(4):
        turn = turn * turn
    closing = 1.0 / (1.0 - turn)
    for part in range(rows // 8):

        def at(node):
            return pl.ds(node * rows + part * 8, 8)

        up = jnp.zeros((8, CZ), f32)
        down = jnp.zeros((8, CZ), f32)
        for node in range(NGY):
            up = up * whole + ends_ref[at(node), :]
            down = down * whole + ends_ref[at(NGY - 1 - node), :]
        up = up * closing
        down = down * closing
        ups, downs = [], [None] * NGY
        for node in range(NGY):
            ups.append(up)
            up = up * whole + ends_ref[at(node), :]
            downs[NGY - 1 - node] = down
            down = down * whole + ends_ref[at(NGY - 1 - node), :]
        for node in range(NGY):
            out_ref[at(node), :] = jnp.where(upward, ups[node], downs[node])


def ring_scan(ranks, ends, own):
    shape = jax.ShapeDtypeStruct(ends.shape, f32)
    return kernel_call(ring_kernel, shape, VMEM, [SMEM, VMEM, VMEM], name="ring_scan")(
        ranks, ends, own
    )


def coefficient_kernel(
    rank_ref, near_ref, far_low_ref, far_high_ref,
    table_ref, green_ref, ends_ref, carry_ref, share_ref, spread_ref, reach_ref, eta_ref,
):
    rank = rank_ref[0]
    lane, row = lanes(), rows_of()
    eta_ref[0:2, :] = far_low_ref[1:3, :]
    eta_ref[2:5, :] = near_ref[0:3, :]
    eta_ref[5:8, :] = far_high_ref[0:3, :]
    eta = pltpu.roll(eta_ref[...], lax.rem(rank + 5, 8), 0)

    def before(x, fill):
        y = pltpu.roll(x, 1, 1)
        return jnp.where(lane == 0, jnp.where(row == 0, fill, pltpu.roll(y, 1, 0)), y)

    def after(x, fill):
        y = pltpu.roll(x, CZ - 1, 1)
        edge = jnp.where(row == NGZ - 1, fill, pltpu.roll(y, NGZ - 1, 0))
        return jnp.where(lane == CZ - 1, edge, y)

    def last_of(x, end):
        return jnp.broadcast_to(x[:, end : end + 1], (8, CZ))

    face_low = z_rate * 0.5 * (before(eta, 0.0) + eta)
    face_high = z_rate * 0.5 * (eta + after(eta, 0.0))

    def pivots(face, up):
        scale = 1.0 / (1.0 + face)
        a = jnp.ones((8, CZ), f32)
        b = face * scale
        c = scale
        d = b
        step = 1
        while step < CZ:
            shift = step if up else CZ - step
            inside = lane >= step if up else lane < CZ - step
            pa, pb, pc, pd = (pltpu.roll(x, shift, 1) for x in (a, b, c, d))
            na, nb = a * pa + b * pc, a * pb + b * pd
            nc, nd = c * pa + d * pc, c * pb + d * pd
            a, b = jnp.where(inside, na, a), jnp.where(inside, nb, b)
            c, d = jnp.where(inside, nc, c), jnp.where(inside, nd, d)
            step *= 2
        end = CZ - 1 if up else 0
        ta, tb, tc, td = (last_of(x, end) for x in (a, b, c, d))
        edge = row == (0 if up else NGZ - 1)
        va, vc = jnp.ones((8, CZ), f32), jnp.zeros((8, CZ), f32)
        for _ in range(NGZ - 1):
            na, nc = ta * va + tb * vc, tc * va + td * vc
            size = 1.0 / (na + nc)
            shift = 1 if up else NGZ - 1
            va = jnp.where(edge, 1.0, pltpu.roll(na * size, shift, 0))
            vc = jnp.where(edge, 0.0, pltpu.roll(nc * size, shift, 0))
        return (a * va + b * vc) / (c * va + d * vc)

    delta_up = pivots(face_low, True)
    delta_down = pivots(face_high, False)
    inverse = 1.0 / (delta_up + delta_down - 1.0)
    first_cell = (lane == 0) & (row == 0)
    last_cell = (lane == CZ - 1) & (row == NGZ - 1)
    link_up = jnp.where(first_cell, 0.0, face_low / (face_low + before(delta_up, 1.0)))
    link_down = jnp.where(last_cell, 0.0, face_high / (face_high + after(delta_down, 1.0)))

    def running(x, up):
        step = 1
        while step < CZ:
            moved = pltpu.roll(x, step if up else CZ - step, 1)
            x = jnp.where(lane >= step if up else lane < CZ - step, x * moved, x)
            step *= 2
        return x

    product_up, product_down = running(link_up, True), running(link_down, False)
    across_up, across_down = last_of(product_up, CZ - 1), last_of(product_down, 0)
    share_up = jnp.zeros((8, CZ), f32)
    share_down = jnp.zeros((8, CZ), f32)
    for _ in range(NGZ - 1):
        moved = pltpu.roll(across_up * share_up, NGZ - 1, 0)
        share_up = jnp.where(row == rank - 1, 1.0, jnp.where(row < rank - 1, moved, 0.0))
        moved = pltpu.roll(across_down * share_down, 1, 0)
        share_down = jnp.where(row == rank + 1, 1.0, jnp.where(row > rank + 1, moved, 0.0))

    def own(x):
        return jnp.sum(jnp.where(row == rank, x, 0.0), axis=0, keepdims=True)

    scale = own(inverse)
    own_up, own_down = own(link_up), own(link_down)
    share_ref[0] = share_up * jnp.broadcast_to(own_up[:, :1], (8, CZ))
    share_ref[1] = share_down * jnp.broadcast_to(own_down[:, CZ - 1 :], (8, CZ))
    lane_1 = lanes((1, CZ))
    within_up = running(jnp.broadcast_to(jnp.where(lane_1 == 0, 1.0, own_up), (8, CZ)), True)
    within_down = running(
        jnp.broadcast_to(jnp.where(lane_1 == CZ - 1, 1.0, own_down), (8, CZ)), False
    )
    square = (CZ, CZ)
    lane_sq, row_sq = lanes(square), rows_of(square)
    carry = jnp.where(
        row_sq < CZ // 2,
        jnp.broadcast_to(within_up[:1] * scale, square),
        jnp.broadcast_to(within_down[:1] * scale, square),
    )
    identity = jnp.where(lane_sq == row_sq, 1.0, 0.0).astype(f32)

    def triangle(link, up):
        link = jnp.where(lanes((1, CZ)) == (0 if up else CZ - 1), 0.0, link)
        link = jnp.broadcast_to(link, (8, CZ))
        out = identity
        step = 1
        while step < CZ:
            shift = step if up else CZ - step
            out = out + jnp.broadcast_to(link[0:1, :], square) * pltpu.roll(out, shift, 1)
            link = link * pltpu.roll(link, shift, 1)
            step *= 2
        return out

    lower, upper = triangle(own_up, True), triangle(own_down, False)
    green = 2.0 * (lower + upper - identity) * jnp.broadcast_to(scale, square)
    ends = 2.0 * jnp.where(
        lane_sq < CZ // 2,
        jnp.broadcast_to(lower[:, CZ - 1 : CZ], square),
        jnp.broadcast_to(upper[:, 0:1], square),
    )
    for matrix, ref in ((green, green_ref), (ends, ends_ref), (carry, carry_ref)):
        for half, part in enumerate(split(matrix)):
            for rows in range(2):
                ref[pl.ds(rows * CZ, CZ), pl.ds(half * CZ, CZ)] = part

    decay, peak = root_of(own(eta))
    y = row_sq & 63
    wide = jnp.broadcast_to(decay, square)
    start = jnp.broadcast_to(peak * decay, square)
    response_up = start * raised(wide, y)
    response_down = start * raised(wide, 63 - y)
    table_ref[0] = response_up[:CY]
    table_ref[1] = response_down[:CY]
    seen = jnp.transpose(ends)
    reach_ref[0] = jnp.transpose(response_up * seen)
    reach_ref[1] = jnp.transpose(response_down * seen)
    y_in, side = flux_place(row_sq)
    low_side = side == 0
    base = jnp.where(
        low_side,
        jnp.broadcast_to(decay[:, :1], square),
        jnp.broadcast_to(decay[:, CZ - 1 :], square),
    )
    top = jnp.where(
        low_side,
        jnp.broadcast_to(peak[:, :1], square),
        jnp.broadcast_to(peak[:, CZ - 1 :], square),
    )
    apart = jnp.abs(y_in - (lane_sq & 63))
    spread = jnp.where(low_side == (lane_sq < CZ // 2), top * raised(base, apart), 0.0)
    spread_ref[0] = 2.0 * spread
    half = row_sq < CZ // 2
    same_y = (lane_sq & 63) == y
    first = jnp.broadcast_to(ends[0:1, :], square)
    final = jnp.broadcast_to(ends[CZ - 1 :, :], square)
    spread_ref[1] = exact_dot(spread, jnp.where(same_y, jnp.where(half, first, final), 0.0))


def coefficients(ranks, near, far_low, far_high):
    matrix = jax.ShapeDtypeStruct((2 * CZ, 2 * CZ), bf16)
    square = jax.ShapeDtypeStruct((2, CZ, CZ), f32)
    return kernel_call(
        coefficient_kernel,
        [
            jax.ShapeDtypeStruct((2, CY, CZ), f32),
            matrix,
            matrix,
            matrix,
            jax.ShapeDtypeStruct((2, NGZ, CZ), f32),
            square,
            square,
        ],
        [VMEM] * 7,
        [SMEM] + [VMEM] * 3,
        [pltpu.VMEM((NGZ, CZ), f32)],
        name="z_coefficients",
        us=3,
    )(ranks, near, far_low, far_high)


def split_rows(left_ref, rows, x):
    high, mid = split(x)
    left_ref[rows, 0:CZ] = high
    left_ref[rows, CZ : 2 * CZ] = mid


def halves(result):
    return result[:, :CZ] + result[:, CZ:]


def fetches_of(u_hbm, m_hbm, u_ref, m_ref, sems):
    def fetches(i):
        return (
            pltpu.make_async_copy(pitched(m_hbm, i), pitched(m_ref, i), sems.at[0, i]),
            pltpu.make_async_copy(chunk(u_hbm, i), chunk(u_ref, i), sems.at[1, i]),
        )

    return fetches


def sums_kernel(m_hbm, u_hbm, ends_ref, sums_ref, m_ref, u_ref, left_ref, sems):
    mask = unit_mask((CY, CZ))

    def work(i):
        for g in range(PER // GROUP):
            left = left_ref.at[g % SLOTS]
            first = i * PER + g * GROUP
            for c in range(GROUP):
                line = first + c
                change = m_ref[pl.ds(line * PITCH, CY), :] - u_ref[line]
                split_rows(left, pl.ds(c * CY, CY), change)
            result = halves(jnp.dot(left[...], ends_ref[...], preferred_element_type=f32))
            for c in range(GROUP):
                part = jnp.where(mask, result[c * CY : (c + 1) * CY], 0.0)
                sums_ref[pl.ds(first + c, 1), :] = jnp.sum(part, axis=0, keepdims=True)

    pipeline(fetches_of(u_hbm, m_hbm, u_ref, m_ref, sems), no_copies, work)


def local_sums(m, u, ends):
    return kernel_call(
        sums_kernel,
        FLAT,
        VMEM,
        [HBM, HBM, VMEM],
        [
            pltpu.VMEM(PITCHED, f32),
            pltpu.VMEM((LINES, CY, CZ), f32),
            pltpu.VMEM((SLOTS, GROUP * CY, 2 * CZ), bf16),
            pltpu.SemaphoreType.DMA((2, STEPS)),
        ],
        name="z_local_sums",
        us=8,
    )(m, u, ends)


def messages_kernel(
    rank_ref, sums_ref, carry_ref, reach_ref, flux_ref, spread_ref, out_ref, layer_ref
):
    rank = rank_ref[0]
    flux = flux_ref[...]
    layer_ref[...] = exact_dot(flux, spread_ref[0])
    sums = sums_ref[...] + exact_dot(flux, spread_ref[1])
    sums = sums + exact_dot(carry_ref[0], reach_ref[0])
    sums = sums + exact_dot(carry_ref[1], reach_ref[1])
    first, second = sums[:ROWS], sums[ROWS:]
    lower = lanes((ROWS, CZ)) < 64
    up = jnp.where(lower, first, pltpu.roll(second, 64, 1))
    down = jnp.where(lower, pltpu.roll(first, 64, 1), second)
    for k in range(NGZ):
        out_ref[k] = jnp.where(rank > k, down, up)


def messages_of(ranks, sums, carries, reach, flux, spread):
    shapes = [jax.ShapeDtypeStruct((NGZ, ROWS, CZ), f32), FLAT]
    call = kernel_call(messages_kernel, shapes, [VMEM] * 2, [SMEM] + [VMEM] * 5, name="z_messages")
    return call(ranks, sums, carries, reach, flux, spread)


def solve_kernel(
    m_hbm, u_hbm, carry_ref, table_ref, green_ref, y_hbm, m_ref, u_ref, y_ref, left_ref, sems
):
    tall = (CY, CZ)

    def stores(i):
        return (pltpu.make_async_copy(chunk(y_ref, i), chunk(y_hbm, i), sems.at[2, i]),)

    def work(i):
        for g in range(PER // GROUP):
            left = left_ref.at[g % SLOTS]
            first = i * PER + g * GROUP
            for c in range(GROUP):
                line = first + c
                carry_up = jnp.broadcast_to(carry_ref[0, pl.ds(line, 1), :], tall)
                carry_down = jnp.broadcast_to(carry_ref[1, pl.ds(line, 1), :], tall)
                change = m_ref[pl.ds(line * PITCH, CY), :] - u_ref[line]
                change = change + table_ref[0] * carry_up + table_ref[1] * carry_down
                split_rows(left, pl.ds(c * CY, CY), change)
            result = halves(jnp.dot(left[...], green_ref[...], preferred_element_type=f32))
            for c in range(GROUP):
                y_ref[first + c] = u_ref[first + c] + result[c * CY : (c + 1) * CY]

    pipeline(fetches_of(u_hbm, m_hbm, u_ref, m_ref, sems), stores, work)


def local_solve(m, u, carries, table, green):
    return kernel_call(
        solve_kernel,
        CUBE,
        HBM,
        [HBM, HBM] + [VMEM] * 3,
        [
            pltpu.VMEM(PITCHED, f32),
            pltpu.VMEM((LINES, CY, CZ), f32),
            pltpu.VMEM((LINES, CY, CZ), f32),
            pltpu.VMEM((SLOTS, GROUP * CY, 2 * CZ), bf16),
            pltpu.SemaphoreType.DMA((3, STEPS)),
        ],
        name="z_local_solve",
        us=8,
    )(m, u, carries, table, green)


def finish_kernel(
    y_hbm, matrix_ref, share_ref, layer_ref, got_ref,
    out_hbm, y_ref, out_ref, left_ref, high_ref, mid_ref, sems,
):
    lower = lanes((ROWS, CZ)) < 64
    tall = (CY, CZ)
    mask = unit_mask(tall)

    def fetches(i):
        return (pltpu.make_async_copy(chunk(y_hbm, i), chunk(y_ref, i), sems.at[0, i]),)

    def stores(i):
        return (pltpu.make_async_copy(chunk(out_ref, i), chunk(out_hbm, i), sems.at[1, i]),)

    def prepare():
        up = jnp.zeros((ROWS, CZ), f32)
        down = jnp.zeros((ROWS, CZ), f32)
        for k in range(NGZ):
            value = got_ref[k]
            up += jnp.broadcast_to(share_ref[0, k : k + 1, :], (ROWS, CZ)) * value
            down += jnp.broadcast_to(share_ref[1, k : k + 1, :], (ROWS, CZ)) * value
        both = (
            jnp.where(lower, up, pltpu.roll(down, 64, 1)),
            jnp.where(lower, pltpu.roll(up, 64, 1), down),
        )
        for half in range(2):
            at = pl.ds(half * ROWS, ROWS)
            high, mid = split(both[half] + layer_ref[at, :])
            high_ref[at, :] = high.astype(f32)
            mid_ref[at, :] = mid.astype(f32)

    def work(i):
        for g in range(PER // GROUP):
            left = left_ref.at[g % SLOTS]
            first = i * PER + g * GROUP
            for c in range(GROUP):
                line = pl.ds(first + c, 1)
                at = pl.ds(c * CY, CY)
                high = jnp.broadcast_to(high_ref[line, :], tall)
                mid = jnp.broadcast_to(mid_ref[line, :], tall)
                left[at, 0:CZ] = jnp.where(mask, high, 0.0).astype(bf16)
                left[at, CZ:] = jnp.where(mask, mid, 0.0).astype(bf16)
            result = halves(jnp.dot(left[...], matrix_ref[...], preferred_element_type=f32))
            for c in range(GROUP):
                out_ref[first + c] = y_ref[first + c] + result[c * CY : (c + 1) * CY]

    pipeline(fetches, stores, work, prepare)


def finish(y, matrix, share, layer, got):
    return kernel_call(
        finish_kernel,
        CUBE,
        HBM,
        [HBM] + [VMEM] * 4,
        [
            pltpu.VMEM((LINES, CY, CZ), f32),
            pltpu.VMEM((LINES, CY, CZ), f32),
            pltpu.VMEM((SLOTS, GROUP * CY, 2 * CZ), bf16),
            pltpu.VMEM((LINES, CZ), f32),
            pltpu.VMEM((LINES, CZ), f32),
            pltpu.SemaphoreType.DMA((2, STEPS)),
        ],
        name="z_carries",
        us=8,
    )(y, matrix, share, layer, got)


def shifted(x, axis, by):
    n = lax.axis_size(axis)
    return lax.ppermute(x, axis, [(i, (i + by) % n) for i in range(n)])


def body(fields, source_term, resistivity):
    u = fields.reshape(LINES, CY, CZ)
    q = source_term.reshape(LINES, CY, CZ)
    ranks = jnp.stack([lax.axis_index("gz"), lax.axis_index("gy")]).astype(jnp.int32)
    own = resistivity.reshape(1, CZ)
    m, ends, columns = sweeps(u, q, own)
    low, high = shifted(columns, "gz", 1), shifted(columns, "gz", -1)
    ends, flux, near = repair(ranks, ends, columns, low, high)
    nodes = lax.all_to_all(ends.reshape(2 * LINES, CZ), "gy", 0, 0, tiled=True)
    far_low, far_high = shifted(near, "gz", 3), shifted(near, "gz", -3)
    table, green, last, vector, share, spread, reach = coefficients(ranks, near, far_low, far_high)
    nodes = ring_scan(ranks, nodes, own)
    carries = lax.all_to_all(nodes, "gy", 0, 0, tiled=True).reshape(2, LINES, CZ)
    sums = local_sums(m, u, last)
    messages, layer = messages_of(ranks, sums, carries, reach, flux, spread)
    got = lax.all_to_all(messages.reshape(NGZ * ROWS, CZ), "gz", 0, 0, tiled=True)
    y = local_solve(m, u, carries, table, green)
    got = got.reshape(NGZ, ROWS, CZ)
    return finish(y, vector, share, layer, got).reshape(fields.shape)


def solution(mesh):
    return jax.shard_map(
        body,
        mesh=mesh,
        in_specs=(P(None, None, "gy", "gz"), P(None, None, "gy", "gz"), P("gz")),
        out_specs=P(None, None, "gy", "gz"),
        check_vma=False,
    )
```

```python
import jax
import jax.numpy as jnp
from jax import lax
from jax.experimental import pallas as pl
from jax.experimental.pallas import tpu as pltpu
from jax.sharding import PartitionSpec as P

f32 = jnp.float32
bf16 = jnp.bfloat16
z_rate = 1.0
y_rate = 0.25

LINES = 192
CY = 64
CZ = 128
GROUP = 8
PER = 32
STEPS = LINES // PER
SLOTS = 2
AHEAD = 3
PITCH = 65
NGY = 16
NGZ = 8


def lanes(shape=(8, CZ)):
    return lax.broadcasted_iota(jnp.int32, shape, len(shape) - 1)


def rows_of(shape=(8, CZ)):
    return lax.broadcasted_iota(jnp.int32, shape, 0)


def root_of(eta):
    k = y_rate * eta
    root = jnp.sqrt(1.0 + 4.0 * k)
    return 2.0 * k / (1.0 + 2.0 * k + root), 1.0 / root


def power_64(r):
    for _ in range(6):
        r = r * r
    return r


def split(x):
    high = x.astype(bf16)
    return high, (x - high.astype(f32)).astype(bf16)


def paired(x):
    high, mid = split(x)
    row = jnp.concatenate([high, mid], axis=1)
    return jnp.concatenate([row, row], axis=0)


def pair_dot(x, matrix):
    high, mid = split(x)
    result = jnp.dot(
        jnp.concatenate([high, mid], axis=1), matrix, preferred_element_type=f32
    )
    half = result.shape[1] // 2
    return result[:, :half] + result[:, half:]


def chunk(ref, step):
    return ref.at[pl.ds(step * PER, PER)]


def kernel_call(kernel, out_shape, out_specs, in_specs, scratch=(), name=None, us=1, mib=8):
    return pl.pallas_call(
        kernel,
        in_specs=in_specs,
        out_specs=out_specs,
        out_shape=out_shape,
        scratch_shapes=list(scratch),
        compiler_params=pltpu.CompilerParams(vmem_limit_bytes=mib * 1024 * 1024),
        cost_estimate=pl.CostEstimate(flops=0, bytes_accessed=us * 3_000_000, transcendentals=0),
        name=name,
    )


def pipeline(fetches, stores, work, prepare=None):
    for i in range(AHEAD):
        for copy in fetches(i):
            copy.start()
    if prepare:
        prepare()

    def step(i, _):
        @pl.when(i + AHEAD < STEPS)
        def _():
            for copy in fetches(i + AHEAD):
                copy.start()

        for copy in fetches(i):
            copy.wait()
        work(i)
        for copy in stores(i):
            copy.start()
        return 0

    lax.fori_loop(0, STEPS, step, 0)

    def drain(i, _):
        for copy in stores(i):
            copy.wait()
        return 0

    lax.fori_loop(0, STEPS, drain, 0)


def pitched(ref, step):
    return ref.at[pl.ds(step * PER * PITCH, PER * PITCH)]


def no_copies(i):
    return ()


def unit_mask(tall):
    return (lanes(tall) & 63) == rows_of(tall)


VMEM = pl.BlockSpec(memory_space=pltpu.VMEM)
SMEM = pl.BlockSpec(memory_space=pltpu.SMEM)
HBM = pl.BlockSpec(memory_space=pltpu.HBM)
CUBE = jax.ShapeDtypeStruct((LINES, CY, CZ), f32)
FLAT = jax.ShapeDtypeStruct((LINES, CZ), f32)
PITCHED = (LINES * PITCH, CZ)
ROWS = LINES // 2
HALO = jax.ShapeDtypeStruct((ROWS, CZ), f32)


def sweep_kernel(
    u_hbm, q_hbm, eta_ref, m_hbm, ends_ref, columns_ref, up_ref, down_ref,
    u_ref, q_ref, m_ref, x_buf, f_buf, sems,
):
    lane = lanes()
    place = ((lane + 1) >> 1) & 63

    def fetches(i):
        return (
            pltpu.make_async_copy(chunk(u_hbm, i), chunk(u_ref, i), sems.at[0, i]),
            pltpu.make_async_copy(chunk(q_hbm, i), chunk(q_ref, i), sems.at[1, i]),
        )

    def stores(i):
        return (pltpu.make_async_copy(pitched(m_ref, i), pitched(m_hbm, i), sems.at[2, i]),)

    eta = jnp.broadcast_to(eta_ref[...], (8, CZ))
    face_low = jnp.where(lane == 0, 0.0, z_rate * 0.5 * (pltpu.roll(eta, 1, 1) + eta))
    face_high = jnp.where(lane == CZ - 1, 0.0, z_rate * 0.5 * (eta + pltpu.roll(eta, CZ - 1, 1)))
    decay, peak = root_of(eta)
    groups = PER // GROUP

    size = PER * PITCH
    half = CY // 2

    def rows(i, g):
        return pl.ds(pl.multiple_of(i * PER + g * GROUP, 8), GROUP)

    def right_side(i, tiles, acc):
        for tile in tiles:
            g, k = tile // 64, tile % 64
            c, at = tile // 8, pl.ds((tile % 8) * 8, 8)
            here = u_ref[i * PER + c, at, :]
            under = pltpu.roll(here, 1, 1)
            over = pltpu.roll(here, CZ - 1, 1)
            acc = jnp.where(place == k, pltpu.roll(here, 2 * k, 1) if k else here, acc)
            q = q_ref[i * PER + c, at, :].astype(f32)
            explicit = face_high * (over - here) - face_low * (here - under)
            x_buf[pl.ds((i % 2) * size + c * PITCH + (tile % 8) * 8, 8), :] = here + explicit + q
            if k == 63:
                columns_ref[rows(i, g), :] = acc
        return acc

    def sweep(i, ahead):
        def x_at(g, y):
            return x_buf[pl.ds((i % 2) * size + g * GROUP * PITCH + y, GROUP, stride=PITCH), :]

        def at(g, y):
            return pl.ds(g * GROUP * PITCH + y, GROUP, stride=PITCH)

        def out(g, y):
            return pl.ds(i * size + g * GROUP * PITCH + y, GROUP, stride=PITCH)

        acc = jnp.zeros((8, CZ), f32)
        forth = [acc] * groups
        back = [acc] * groups
        for s in range(CY):
            low, high = s, CY - 1 - s
            for g in range(groups):
                forth[g] = forth[g] * decay + x_at(g, low)
                kept = back[g] * decay
                back[g] = kept + x_at(g, high)
                if s < half:
                    f_buf[at(g, low), :] = forth[g]
                    f_buf[at(g, high), :] = kept
                else:
                    m_ref[out(g, low), :] = peak * (forth[g] + f_buf[at(g, low), :])
                    m_ref[out(g, high), :] = peak * (f_buf[at(g, high), :] + kept)
            if ahead:
                each = PER * CY // 8 // CY
                acc = right_side(i + 1, range(s * each, (s + 1) * each), acc)
        for g in range(groups):
            ends_ref[0, rows(i, g), :] = forth[g]
            ends_ref[1, rows(i, g), :] = back[g]

    for i in range(AHEAD):
        for copy in fetches(i):
            copy.start()
    for copy in fetches(0):
        copy.wait()
    right_side(0, range(PER * CY // 8), jnp.zeros((8, CZ), f32))

    def step(i, _):
        @pl.when(i + AHEAD < STEPS)
        def _():
            for copy in fetches(i + AHEAD):
                copy.start()

        for copy in fetches(i + 1):
            copy.wait()
        sweep(i, True)
        for copy in stores(i):
            copy.start()
        return 0

    lax.fori_loop(0, STEPS - 1, step, 0)
    sweep(STEPS - 1, False)
    for copy in stores(STEPS - 1):
        copy.start()
    for i in range(STEPS):
        for copy in stores(i):
            copy.wait()
    first, second = columns_ref[:ROWS], columns_ref[ROWS:]
    odd = lanes((ROWS, CZ)) & 1 == 1
    up_ref[...] = jnp.where(odd, first, pltpu.roll(second, 1, 1))
    down_ref[...] = jnp.where(odd, pltpu.roll(second, CZ - 1, 1), first)


def sweeps(u, q, own):
    return kernel_call(
        sweep_kernel,
        [
            jax.ShapeDtypeStruct(PITCHED, f32),
            jax.ShapeDtypeStruct((2, LINES, CZ), f32),
            FLAT,
            HALO,
            HALO,
        ],
        [HBM] + [VMEM] * 4,
        [HBM, HBM, VMEM],
        [
            pltpu.VMEM((LINES, CY, CZ), f32),
            pltpu.VMEM((LINES, CY, CZ), bf16),
            pltpu.VMEM(PITCHED, f32),
            pltpu.VMEM((2 * PER * PITCH, CZ), f32),
            pltpu.VMEM((PER * PITCH, CZ), f32),
            pltpu.SemaphoreType.DMA((3, STEPS)),
        ],
        name="y_sweeps",
        mib=51,
        us=12,
    )(u, q, own)


def raised(base, exponent, bits=6):
    out = jnp.ones_like(base)
    for bit in range(bits):
        out = jnp.where((exponent >> bit) & 1 == 1, out * base, out)
        base = base * base
    return out


def flux_place(l):
    return 8 * ((l >> 1) & 7) + (l >> 4), l & 1


def turned(x):
    lane, row = lanes(x.shape), rows_of(x.shape)
    for bit in range(3):
        rows, columns = 1 << bit, 16 << bit
        in_row, in_lane = (row >> bit) & 1, (lane >> (4 + bit)) & 1
        count = x.shape[0]
        forth = pltpu.roll(pltpu.roll(x, count - rows, 0), columns, 1)
        back = pltpu.roll(pltpu.roll(x, rows, 0), CZ - columns, 1)
        x = jnp.where(in_row == in_lane, x, jnp.where(in_row == 0, forth, back))
    return x


def repair_kernel(
    rank_ref, ends_ref, columns_ref, low_ref, high_ref, face_ref, repair_ref, out_ref, flux_ref
):
    rank = rank_ref[0]
    even = lanes((ROWS, CZ)) & 1 == 0
    face = jnp.broadcast_to(face_ref[:1], (ROWS, CZ))
    low = jnp.where(rank > 0, low_ref[...], 0.0)
    high = jnp.where(rank < NGZ - 1, high_ref[...], 0.0)
    outer = (
        jnp.where(even, pltpu.roll(low, 1, 1), pltpu.roll(high, 1, 1)),
        jnp.where(even, low, pltpu.roll(high, 2, 1)),
    )
    for half in range(2):
        at = pl.ds(half * ROWS, ROWS)
        columns = columns_ref[at, :]
        inner = jnp.where(even, columns, pltpu.roll(columns, 2, 1))
        flux = turned(face * (outer[half] - inner))
        flux_ref[at, :] = flux
        added = pair_dot(flux, repair_ref[...])
        out_ref[0, at, :] = ends_ref[0, at, :] + added[:, :CZ]
        out_ref[1, at, :] = ends_ref[1, at, :] + added[:, CZ:]


def repair(ranks, ends, columns, low, high, face, matrix):
    shapes = [jax.ShapeDtypeStruct((2, LINES, CZ), f32), FLAT]
    call = kernel_call(repair_kernel, shapes, [VMEM] * 2, [SMEM] + [VMEM] * 6, name="repair")
    return call(ranks, ends, columns, low, high, face, matrix)


def ring_kernel(rank_ref, ends_ref, turn_ref, out_ref):
    rows = 2 * LINES // NGY
    upward = rank_ref[1] < NGY // 2
    whole, closing = turn_ref[0], turn_ref[1]
    for part in range(rows // 8):

        def at(node):
            return pl.ds(node * rows + part * 8, 8)

        up = jnp.zeros((8, CZ), f32)
        down = jnp.zeros((8, CZ), f32)
        for node in range(NGY):
            up = up * whole + ends_ref[at(node), :]
            down = down * whole + ends_ref[at(NGY - 1 - node), :]
        up = up * closing
        down = down * closing
        ups, downs = [], [None] * NGY
        for node in range(NGY):
            ups.append(up)
            up = up * whole + ends_ref[at(node), :]
            downs[NGY - 1 - node] = down
            down = down * whole + ends_ref[at(NGY - 1 - node), :]
        for node in range(NGY):
            out_ref[at(node), :] = jnp.where(upward, ups[node], downs[node])


def ring_scan(ranks, ends, turn):
    shape = jax.ShapeDtypeStruct(ends.shape, f32)
    return kernel_call(ring_kernel, shape, VMEM, [SMEM, VMEM, VMEM], name="ring_scan")(
        ranks, ends, turn
    )


def coefficient_kernel(
    rank_ref, eta_ref, face_ref, repair_ref, table_ref,
    turn_ref, green_ref, ends_ref, carry_ref, share_ref, layer_ref, reach_ref,
):
    rank = rank_ref[0]
    lane, row = lanes(), rows_of()
    eta = eta_ref[...]

    def before(x, fill):
        y = pltpu.roll(x, 1, 1)
        return jnp.where(lane == 0, jnp.where(row == 0, fill, pltpu.roll(y, 1, 0)), y)

    def after(x, fill):
        y = pltpu.roll(x, CZ - 1, 1)
        edge = jnp.where(row == NGZ - 1, fill, pltpu.roll(y, NGZ - 1, 0))
        return jnp.where(lane == CZ - 1, edge, y)

    def last_of(x, end):
        return jnp.broadcast_to(x[:, end : end + 1], (8, CZ))

    face_low = z_rate * 0.5 * (before(eta, 0.0) + eta)
    face_high = z_rate * 0.5 * (eta + after(eta, 0.0))

    def pivots(face, up):
        scale = 1.0 / (1.0 + face)
        a = jnp.ones((8, CZ), f32)
        b = face * scale
        c = scale
        d = b
        step = 1
        while step < CZ:
            shift = step if up else CZ - step
            inside = lane >= step if up else lane < CZ - step
            pa, pb, pc, pd = (pltpu.roll(x, shift, 1) for x in (a, b, c, d))
            na, nb = a * pa + b * pc, a * pb + b * pd
            nc, nd = c * pa + d * pc, c * pb + d * pd
            a, b = jnp.where(inside, na, a), jnp.where(inside, nb, b)
            c, d = jnp.where(inside, nc, c), jnp.where(inside, nd, d)
            step *= 2
        end = CZ - 1 if up else 0
        ta, tb, tc, td = (last_of(x, end) for x in (a, b, c, d))
        edge = row == (0 if up else NGZ - 1)
        va, vc = jnp.ones((8, CZ), f32), jnp.zeros((8, CZ), f32)
        for _ in range(NGZ - 1):
            na, nc = ta * va + tb * vc, tc * va + td * vc
            size = 1.0 / (na + nc)
            shift = 1 if up else NGZ - 1
            va = jnp.where(edge, 1.0, pltpu.roll(na * size, shift, 0))
            vc = jnp.where(edge, 0.0, pltpu.roll(nc * size, shift, 0))
        return (a * va + b * vc) / (c * va + d * vc)

    delta_up = pivots(face_low, True)
    delta_down = pivots(face_high, False)
    inverse = 1.0 / (delta_up + delta_down - 1.0)
    first_cell = (lane == 0) & (row == 0)
    last_cell = (lane == CZ - 1) & (row == NGZ - 1)
    link_up = jnp.where(first_cell, 0.0, face_low / (face_low + before(delta_up, 1.0)))
    link_down = jnp.where(last_cell, 0.0, face_high / (face_high + after(delta_down, 1.0)))

    def running(x, up):
        step = 1
        while step < CZ:
            moved = pltpu.roll(x, step if up else CZ - step, 1)
            x = jnp.where(lane >= step if up else lane < CZ - step, x * moved, x)
            step *= 2
        return x

    product_up, product_down = running(link_up, True), running(link_down, False)
    across_up, across_down = last_of(product_up, CZ - 1), last_of(product_down, 0)
    share_up = jnp.zeros((8, CZ), f32)
    share_down = jnp.zeros((8, CZ), f32)
    for _ in range(NGZ - 1):
        moved = pltpu.roll(across_up * share_up, NGZ - 1, 0)
        share_up = jnp.where(row == rank - 1, 1.0, jnp.where(row < rank - 1, moved, 0.0))
        moved = pltpu.roll(across_down * share_down, 1, 0)
        share_down = jnp.where(row == rank + 1, 1.0, jnp.where(row > rank + 1, moved, 0.0))

    def own(x):
        return jnp.sum(jnp.where(row == rank, x, 0.0), axis=0, keepdims=True)

    scale = own(inverse)
    own_up, own_down = own(link_up), own(link_down)
    share_ref[0] = share_up * jnp.broadcast_to(own_up[:, :1], (8, CZ))
    share_ref[1] = share_down * jnp.broadcast_to(own_down[:, CZ - 1 :], (8, CZ))
    lane_1 = lanes((1, CZ))
    within_up = running(jnp.broadcast_to(jnp.where(lane_1 == 0, 1.0, own_up), (8, CZ)), True)
    within_down = running(
        jnp.broadcast_to(jnp.where(lane_1 == CZ - 1, 1.0, own_down), (8, CZ)), False
    )
    square = (CZ, CZ)
    lane_sq, row_sq = lanes(square), rows_of(square)
    carry = jnp.where(
        row_sq < CZ // 2,
        jnp.broadcast_to(within_up[:1] * scale, square),
        jnp.broadcast_to(within_down[:1] * scale, square),
    )
    identity = jnp.where(lane_sq == row_sq, 1.0, 0.0).astype(f32)

    def triangle(link, up):
        link = jnp.where(lanes((1, CZ)) == (0 if up else CZ - 1), 0.0, link)
        link = jnp.broadcast_to(link, (8, CZ))
        out = identity
        step = 1
        while step < CZ:
            shift = step if up else CZ - step
            out = out + jnp.broadcast_to(link[0:1, :], square) * pltpu.roll(out, shift, 1)
            link = link * pltpu.roll(link, shift, 1)
            step *= 2
        return out

    lower, upper = triangle(own_up, True), triangle(own_down, False)
    green = 2.0 * (lower + upper - identity) * jnp.broadcast_to(scale, square)
    ends = 2.0 * jnp.where(
        lane_sq < CZ // 2,
        jnp.broadcast_to(lower[:, CZ - 1 : CZ], square),
        jnp.broadcast_to(upper[:, 0:1], square),
    )
    for matrix, ref in ((green, green_ref), (ends, ends_ref), (carry, carry_ref)):
        ref[...] = paired(matrix)

    decay, peak = root_of(own(eta))
    whole = power_64(jnp.broadcast_to(decay, (8, CZ)))
    around = whole
    for _ in range(4):
        around = around * around
    turn_ref[0] = whole
    turn_ref[1] = 1.0 / (1.0 - around)
    y = row_sq & 63
    wide = jnp.broadcast_to(decay, square)
    start = jnp.broadcast_to(peak * decay, square)
    seen = jnp.transpose(ends)
    reach = []
    for way in range(2):
        response = start * raised(wide, (y, CY - 1 - y)[way])
        table_ref[way] = response[:CY]
        reach.append(jnp.transpose(response * seen))
    reach_ref[...] = paired(jnp.concatenate(reach, axis=0))
    y, side = flux_place(row_sq)
    low = side == 0

    def sided(x):
        return jnp.where(
            low, jnp.broadcast_to(x[:, :1], square), jnp.broadcast_to(x[:, CZ - 1 :], square)
        )

    face = jnp.where(
        lane_1 & 1 == 0,
        jnp.broadcast_to(own(face_low)[:, :1], (1, CZ)),
        jnp.broadcast_to(own(face_high)[:, CZ - 1 :], (1, CZ)),
    )
    face_ref[...] = jnp.broadcast_to(face, (8, CZ))
    base = sided(decay)
    place = lane_sq == jnp.where(low, 0, CZ - 1)
    forth = jnp.where(place, raised(base, CY - 1 - y), 0.0)
    back = jnp.where(place, raised(base, y), 0.0)
    repair_ref[...] = paired(jnp.concatenate([forth, back], axis=1))
    apart = jnp.abs(y - (lane_sq & 63))
    spread = jnp.where(low == (lane_sq < 64), sided(peak) * raised(base, apart), 0.0)
    same_y = (lane_sq & 63) == (row_sq & 63)
    first = jnp.broadcast_to(ends[0:1, :], square)
    final = jnp.broadcast_to(ends[CZ - 1 :, :], square)
    layer = jnp.where(same_y, jnp.where(row_sq < 64, first, final), 0.0)
    layer_ref[...] = paired(jnp.concatenate([2.0 * spread, pair_dot(spread, paired(layer))], axis=1))


def coefficients(ranks, etas):
    def matrix(rows, columns):
        return jax.ShapeDtypeStruct((2 * rows * CZ, 2 * columns * CZ), bf16)

    return kernel_call(
        coefficient_kernel,
        [
            jax.ShapeDtypeStruct((8, CZ), f32),
            matrix(1, 2),
            jax.ShapeDtypeStruct((2, CY, CZ), f32),
            jax.ShapeDtypeStruct((2, 8, CZ), f32),
            matrix(1, 1),
            matrix(1, 1),
            matrix(1, 1),
            jax.ShapeDtypeStruct((2, NGZ, CZ), f32),
            matrix(1, 2),
            matrix(2, 1),
        ],
        [VMEM] * 10,
        [SMEM, VMEM],
        name="z_coefficients",
        us=4,
    )(ranks, etas)


def split_rows(left_ref, rows, x):
    high, mid = split(x)
    left_ref[rows, 0:CZ] = high
    left_ref[rows, CZ : 2 * CZ] = mid


def halves(result):
    return result[:, :CZ] + result[:, CZ:]


def fetches_of(u_hbm, m_hbm, u_ref, m_ref, sems):
    def fetches(i):
        return (
            pltpu.make_async_copy(pitched(m_hbm, i), pitched(m_ref, i), sems.at[0, i]),
            pltpu.make_async_copy(chunk(u_hbm, i), chunk(u_ref, i), sems.at[1, i]),
        )

    return fetches


def sums_kernel(
    m_hbm, u_hbm, ends_ref, flux_ref, spread_ref, sums_ref, layer_ref, m_ref, u_ref, left_ref, seen_ref, sems
):
    mask = unit_mask((CY, CZ))

    def prepare():
        both = pair_dot(flux_ref[...], spread_ref[...])
        layer_ref[...] = both[:, :CZ]
        seen_ref[...] = both[:, CZ:]

    def work(i):
        for g in range(PER // GROUP):
            left = left_ref.at[g % SLOTS]
            first = i * PER + g * GROUP
            for c in range(GROUP):
                line = first + c
                change = m_ref[pl.ds(line * PITCH, CY), :] - u_ref[line]
                split_rows(left, pl.ds(c * CY, CY), change)
            result = halves(jnp.dot(left[...], ends_ref[...], preferred_element_type=f32))
            for c in range(GROUP):
                part = jnp.where(mask, result[c * CY : (c + 1) * CY], 0.0)
                sums_ref[pl.ds(first + c, 1), :] = jnp.sum(part, axis=0, keepdims=True)

    pipeline(fetches_of(u_hbm, m_hbm, u_ref, m_ref, sems), no_copies, work, prepare)
    sums_ref[...] += seen_ref[...]


def local_sums(m, u, ends, flux, spread):
    return kernel_call(
        sums_kernel,
        [FLAT, FLAT],
        [VMEM] * 2,
        [HBM, HBM] + [VMEM] * 3,
        [
            pltpu.VMEM(PITCHED, f32),
            pltpu.VMEM((LINES, CY, CZ), f32),
            pltpu.VMEM((SLOTS, GROUP * CY, 2 * CZ), bf16),
            pltpu.VMEM((LINES, CZ), f32),
            pltpu.SemaphoreType.DMA((2, STEPS)),
        ],
        name="z_local_sums",
        mib=48,
        us=8,
    )(m, u, ends, flux, spread)


def messages_kernel(rank_ref, sums_ref, carry_ref, reach_ref, out_ref):
    rank = rank_ref[0]
    carries = jnp.concatenate([carry_ref[0], carry_ref[1]], axis=1)
    sums = sums_ref[...] + pair_dot(carries, reach_ref[...])
    first, second = sums[:ROWS], sums[ROWS:]
    lower = lanes((ROWS, CZ)) < 64
    up = jnp.where(lower, first, pltpu.roll(second, 64, 1))
    down = jnp.where(lower, pltpu.roll(first, 64, 1), second)
    for k in range(NGZ):
        out_ref[k] = jnp.where(rank > k, down, up)


def messages_of(ranks, sums, carries, reach):
    shape = jax.ShapeDtypeStruct((NGZ, ROWS, CZ), f32)
    call = kernel_call(messages_kernel, shape, VMEM, [SMEM] + [VMEM] * 3, name="z_messages")
    return call(ranks, sums, carries, reach)


def solve_kernel(
    m_hbm, u_hbm, carry_ref, table_ref, green_ref, y_hbm, m_ref, u_ref, y_ref, left_ref, sems
):
    tall = (CY, CZ)

    def stores(i):
        return (pltpu.make_async_copy(chunk(y_ref, i), chunk(y_hbm, i), sems.at[2, i]),)

    def work(i):
        for g in range(PER // GROUP):
            left = left_ref.at[g % SLOTS]
            first = i * PER + g * GROUP
            for c in range(GROUP):
                line = first + c
                carry_up = jnp.broadcast_to(carry_ref[0, pl.ds(line, 1), :], tall)
                carry_down = jnp.broadcast_to(carry_ref[1, pl.ds(line, 1), :], tall)
                change = m_ref[pl.ds(line * PITCH, CY), :] - u_ref[line]
                change = change + table_ref[0] * carry_up + table_ref[1] * carry_down
                split_rows(left, pl.ds(c * CY, CY), change)
            result = halves(jnp.dot(left[...], green_ref[...], preferred_element_type=f32))
            for c in range(GROUP):
                y_ref[first + c] = u_ref[first + c] + result[c * CY : (c + 1) * CY]

    pipeline(fetches_of(u_hbm, m_hbm, u_ref, m_ref, sems), stores, work)


def local_solve(m, u, carries, table, green):
    return kernel_call(
        solve_kernel,
        CUBE,
        HBM,
        [HBM, HBM] + [VMEM] * 3,
        [
            pltpu.VMEM(PITCHED, f32),
            pltpu.VMEM((LINES, CY, CZ), f32),
            pltpu.VMEM((LINES, CY, CZ), f32),
            pltpu.VMEM((SLOTS, GROUP * CY, 2 * CZ), bf16),
            pltpu.SemaphoreType.DMA((3, STEPS)),
        ],
        name="z_local_solve",
        mib=48,
        us=8,
    )(m, u, carries, table, green)


def finish_kernel(
    y_hbm, matrix_ref, share_ref, layer_ref, got_ref,
    out_hbm, y_ref, out_ref, left_ref, high_ref, mid_ref, sems,
):
    lower = lanes((ROWS, CZ)) < 64
    tall = (CY, CZ)
    mask = unit_mask(tall)

    def fetches(i):
        return (pltpu.make_async_copy(chunk(y_hbm, i), chunk(y_ref, i), sems.at[0, i]),)

    def stores(i):
        return (pltpu.make_async_copy(chunk(out_ref, i), chunk(out_hbm, i), sems.at[1, i]),)

    def prepare():
        up = jnp.zeros((ROWS, CZ), f32)
        down = jnp.zeros((ROWS, CZ), f32)
        for k in range(NGZ):
            value = got_ref[k]
            up += jnp.broadcast_to(share_ref[0, k : k + 1, :], (ROWS, CZ)) * value
            down += jnp.broadcast_to(share_ref[1, k : k + 1, :], (ROWS, CZ)) * value
        both = (
            jnp.where(lower, up, pltpu.roll(down, 64, 1)),
            jnp.where(lower, pltpu.roll(up, 64, 1), down),
        )
        for half in range(2):
            at = pl.ds(half * ROWS, ROWS)
            high, mid = split(both[half] + layer_ref[at, :])
            high_ref[at, :] = high.astype(f32)
            mid_ref[at, :] = mid.astype(f32)

    def work(i):
        for g in range(PER // GROUP):
            left = left_ref.at[g % SLOTS]
            first = i * PER + g * GROUP
            for c in range(GROUP):
                line = pl.ds(first + c, 1)
                at = pl.ds(c * CY, CY)
                high = jnp.broadcast_to(high_ref[line, :], tall)
                mid = jnp.broadcast_to(mid_ref[line, :], tall)
                left[at, 0:CZ] = jnp.where(mask, high, 0.0).astype(bf16)
                left[at, CZ:] = jnp.where(mask, mid, 0.0).astype(bf16)
            result = halves(jnp.dot(left[...], matrix_ref[...], preferred_element_type=f32))
            for c in range(GROUP):
                out_ref[first + c] = y_ref[first + c] + result[c * CY : (c + 1) * CY]

    pipeline(fetches, stores, work, prepare)


def finish(y, matrix, share, layer, got):
    return kernel_call(
        finish_kernel,
        CUBE,
        HBM,
        [HBM] + [VMEM] * 4,
        [
            pltpu.VMEM((LINES, CY, CZ), f32),
            pltpu.VMEM((LINES, CY, CZ), f32),
            pltpu.VMEM((SLOTS, GROUP * CY, 2 * CZ), bf16),
            pltpu.VMEM((LINES, CZ), f32),
            pltpu.VMEM((LINES, CZ), f32),
            pltpu.SemaphoreType.DMA((2, STEPS)),
        ],
        name="z_carries",
        mib=48,
        us=8,
    )(y, matrix, share, layer, got)


def shifted(x, axis, by):
    n = lax.axis_size(axis)
    return lax.ppermute(x, axis, [(i, (i + by) % n) for i in range(n)])


def body(fields, source_term, resistivity):
    u = fields.reshape(LINES, CY, CZ)
    q = source_term.reshape(LINES, CY, CZ)
    ranks = jnp.stack([lax.axis_index("gz"), lax.axis_index("gy")]).astype(jnp.int32)
    own = resistivity.reshape(1, CZ)
    etas = lax.all_to_all(jnp.broadcast_to(own, (NGZ, CZ)), "gz", 0, 0, tiled=True)
    m, ends, columns, up, down = sweeps(u, q, own)
    low, high = shifted(up, "gz", 1), shifted(down, "gz", -1)
    face, matrix, table, turn, green, last, vector, share, layers, reach = coefficients(ranks, etas)
    ends, flux = repair(ranks, ends, columns, low, high, face, matrix)
    nodes = lax.all_to_all(ends.reshape(2 * LINES, CZ), "gy", 0, 0, tiled=True)
    nodes = ring_scan(ranks, nodes, turn)
    carries = lax.all_to_all(nodes, "gy", 0, 0, tiled=True).reshape(2, LINES, CZ)
    sums, layer = local_sums(m, u, last, flux, layers)
    messages = messages_of(ranks, sums, carries, reach)
    got = lax.all_to_all(messages.reshape(NGZ * ROWS, CZ), "gz", 0, 0, tiled=True)
    y = local_solve(m, u, carries, table, green)
    got = got.reshape(NGZ, ROWS, CZ)
    return finish(y, vector, share, layer, got).reshape(fields.shape)


def solution(mesh):
    return jax.shard_map(
        body,
        mesh=mesh,
        in_specs=(P(None, None, "gy", "gz"), P(None, None, "gy", "gz"), P("gz")),
        out_specs=P(None, None, "gy", "gz"),
        check_vma=False,
    )
```

```python
import jax
import jax.numpy as jnp
from jax import lax
from jax.experimental import pallas as pl
from jax.experimental.pallas import tpu as pltpu
from jax.sharding import PartitionSpec as P

f32 = jnp.float32
bf16 = jnp.bfloat16
z_rate = 1.0
y_rate = 0.25

LINES = 192
CY = 64
CZ = 128
GROUP = 8
PER = 32
STEPS = LINES // PER
SLOTS = 2
AHEAD = 3
PITCH = 65
NGY = 16
NGZ = 8


def lanes(shape=(8, CZ)):
    return lax.broadcasted_iota(jnp.int32, shape, len(shape) - 1)


def rows_of(shape=(8, CZ)):
    return lax.broadcasted_iota(jnp.int32, shape, 0)


def root_of(eta):
    k = y_rate * eta
    root = jnp.sqrt(1.0 + 4.0 * k)
    return 2.0 * k / (1.0 + 2.0 * k + root), 1.0 / root


def power_64(r):
    for _ in range(6):
        r = r * r
    return r


def split(x):
    high = x.astype(bf16)
    return high, (x - high.astype(f32)).astype(bf16)


def paired(x):
    high, mid = split(x)
    row = jnp.concatenate([high, mid], axis=1)
    return jnp.concatenate([row, row], axis=0)


def pair_dot(x, matrix):
    high, mid = split(x)
    result = jnp.dot(
        jnp.concatenate([high, mid], axis=1), matrix, preferred_element_type=f32
    )
    half = result.shape[1] // 2
    return result[:, :half] + result[:, half:]


def chunk(ref, step):
    return ref.at[pl.ds(step * PER, PER)]


def kernel_call(kernel, out_shape, out_specs, in_specs, scratch=(), name=None, us=1, mib=8):
    return pl.pallas_call(
        kernel,
        in_specs=in_specs,
        out_specs=out_specs,
        out_shape=out_shape,
        scratch_shapes=list(scratch),
        compiler_params=pltpu.CompilerParams(vmem_limit_bytes=mib * 1024 * 1024),
        cost_estimate=pl.CostEstimate(flops=0, bytes_accessed=us * 3_000_000, transcendentals=0),
        name=name,
    )


def pipeline(fetches, stores, work, prepare=None):
    for i in range(AHEAD):
        for copy in fetches(i):
            copy.start()
    if prepare:
        prepare()

    def step(i, _):
        @pl.when(i + AHEAD < STEPS)
        def _():
            for copy in fetches(i + AHEAD):
                copy.start()

        for copy in fetches(i):
            copy.wait()
        work(i)
        for copy in stores(i):
            copy.start()
        return 0

    lax.fori_loop(0, STEPS, step, 0)

    def drain(i, _):
        for copy in stores(i):
            copy.wait()
        return 0

    lax.fori_loop(0, STEPS, drain, 0)


def pitched(ref, step):
    return ref.at[pl.ds(step * PER * PITCH, PER * PITCH)]


def no_copies(i):
    return ()


def unit_mask(tall):
    return (lanes(tall) & 63) == rows_of(tall)


VMEM = pl.BlockSpec(memory_space=pltpu.VMEM)
SMEM = pl.BlockSpec(memory_space=pltpu.SMEM)
HBM = pl.BlockSpec(memory_space=pltpu.HBM)
CUBE = jax.ShapeDtypeStruct((LINES, CY, CZ), f32)
FLAT = jax.ShapeDtypeStruct((LINES, CZ), f32)
PITCHED = (LINES * PITCH, CZ)
ROWS = LINES // 2
HALO = jax.ShapeDtypeStruct((ROWS + 8, CZ), f32)


def sweep_kernel(
    u_hbm, q_hbm, eta_hbm, m_hbm, ends_ref, columns_ref, up_ref, down_ref,
    u_ref, q_ref, m_ref, x_buf, f_buf, eta_ref, eta_sem, sems,
):
    lane = lanes()
    place = ((lane + 1) >> 1) & 63

    def fetches(i):
        return (
            pltpu.make_async_copy(chunk(u_hbm, i), chunk(u_ref, i), sems.at[0, i]),
            pltpu.make_async_copy(chunk(q_hbm, i), chunk(q_ref, i), sems.at[1, i]),
        )

    def stores(i):
        return (pltpu.make_async_copy(pitched(m_ref, i), pitched(m_hbm, i), sems.at[2, i]),)

    eta_copy = pltpu.make_async_copy(eta_hbm, eta_ref, eta_sem)
    eta_copy.start()
    for i in range(AHEAD):
        for copy in fetches(i):
            copy.start()
    eta_copy.wait()
    eta = jnp.broadcast_to(eta_ref[...], (8, CZ))
    up_ref[pl.ds(ROWS, 8), :] = eta
    down_ref[pl.ds(ROWS, 8), :] = eta
    face_low = jnp.where(lane == 0, 0.0, z_rate * 0.5 * (pltpu.roll(eta, 1, 1) + eta))
    face_high = jnp.where(lane == CZ - 1, 0.0, z_rate * 0.5 * (eta + pltpu.roll(eta, CZ - 1, 1)))
    decay, peak = root_of(eta)
    groups = PER // GROUP

    size = PER * PITCH
    half = CY // 2

    def rows(i, g):
        return pl.ds(pl.multiple_of(i * PER + g * GROUP, 8), GROUP)

    def right_side(i, tiles, acc):
        for tile in tiles:
            g, k = tile // 64, tile % 64
            c, at = tile // 8, pl.ds((tile % 8) * 8, 8)
            here = u_ref[i * PER + c, at, :]
            under = pltpu.roll(here, 1, 1)
            over = pltpu.roll(here, CZ - 1, 1)
            acc = jnp.where(place == k, pltpu.roll(here, 2 * k, 1) if k else here, acc)
            q = q_ref[i * PER + c, at, :].astype(f32)
            explicit = face_high * (over - here) - face_low * (here - under)
            x_buf[pl.ds((i % 2) * size + c * PITCH + (tile % 8) * 8, 8), :] = here + explicit + q
            if k == 63:
                columns_ref[rows(i, g), :] = acc
        return acc

    def sweep(i, ahead):
        def x_at(g, y):
            return x_buf[pl.ds((i % 2) * size + g * GROUP * PITCH + y, GROUP, stride=PITCH), :]

        def at(g, y):
            return pl.ds(g * GROUP * PITCH + y, GROUP, stride=PITCH)

        def out(g, y):
            return pl.ds(i * size + g * GROUP * PITCH + y, GROUP, stride=PITCH)

        acc = jnp.zeros((8, CZ), f32)
        forth = [acc] * groups
        back = [acc] * groups
        for s in range(CY):
            low, high = s, CY - 1 - s
            for g in range(groups):
                forth[g] = forth[g] * decay + x_at(g, low)
                kept = back[g] * decay
                back[g] = kept + x_at(g, high)
                if s < half:
                    f_buf[at(g, low), :] = forth[g]
                    f_buf[at(g, high), :] = kept
                else:
                    m_ref[out(g, low), :] = peak * (forth[g] + f_buf[at(g, low), :])
                    m_ref[out(g, high), :] = peak * (f_buf[at(g, high), :] + kept)
            if ahead:
                each = PER * CY // 8 // CY
                acc = right_side(i + 1, range(s * each, (s + 1) * each), acc)
        for g in range(groups):
            ends_ref[0, rows(i, g), :] = forth[g]
            ends_ref[1, rows(i, g), :] = back[g]

    for copy in fetches(0):
        copy.wait()
    right_side(0, range(PER * CY // 8), jnp.zeros((8, CZ), f32))

    def step(i, _):
        @pl.when(i + AHEAD < STEPS)
        def _():
            for copy in fetches(i + AHEAD):
                copy.start()

        for copy in fetches(i + 1):
            copy.wait()
        sweep(i, True)
        for copy in stores(i):
            copy.start()
        return 0

    lax.fori_loop(0, STEPS - 1, step, 0)
    sweep(STEPS - 1, False)
    for copy in stores(STEPS - 1):
        copy.start()
    for i in range(STEPS):
        for copy in stores(i):
            copy.wait()
    first, second = columns_ref[:ROWS], columns_ref[ROWS:]
    odd = lanes((ROWS, CZ)) & 1 == 1
    up_ref[:ROWS] = jnp.where(odd, first, pltpu.roll(second, 1, 1))
    down_ref[:ROWS] = jnp.where(odd, pltpu.roll(second, CZ - 1, 1), first)


def sweeps(u, q, own):
    return kernel_call(
        sweep_kernel,
        [
            jax.ShapeDtypeStruct(PITCHED, f32),
            jax.ShapeDtypeStruct((2, LINES, CZ), f32),
            FLAT,
            HALO,
            HALO,
        ],
        [HBM] + [VMEM] * 4,
        [HBM] * 3,
        [
            pltpu.VMEM((LINES, CY, CZ), f32),
            pltpu.VMEM((LINES, CY, CZ), bf16),
            pltpu.VMEM(PITCHED, f32),
            pltpu.VMEM((2 * PER * PITCH, CZ), f32),
            pltpu.VMEM((PER * PITCH, CZ), f32),
            pltpu.VMEM((1, CZ), f32),
            pltpu.SemaphoreType.DMA,
            pltpu.SemaphoreType.DMA((3, STEPS)),
        ],
        name="y_sweeps",
        mib=51,
        us=12,
    )(u, q, own)


def raised(base, exponent, bits=6):
    out = jnp.ones_like(base)
    for bit in range(bits):
        out = jnp.where((exponent >> bit) & 1 == 1, out * base, out)
        base = base * base
    return out


def flux_place(l):
    return 8 * ((l >> 1) & 7) + (l >> 4), l & 1


def turned(x):
    lane, row = lanes(x.shape), rows_of(x.shape)
    for bit in range(3):
        rows, columns = 1 << bit, 16 << bit
        in_row, in_lane = (row >> bit) & 1, (lane >> (4 + bit)) & 1
        count = x.shape[0]
        forth = pltpu.roll(pltpu.roll(x, count - rows, 0), columns, 1)
        back = pltpu.roll(pltpu.roll(x, rows, 0), CZ - columns, 1)
        x = jnp.where(in_row == in_lane, x, jnp.where(in_row == 0, forth, back))
    return x


def sided_by(low):
    def sided(x):
        return jnp.where(
            low, jnp.broadcast_to(x[:, :1], low.shape), jnp.broadcast_to(x[:, CZ - 1 :], low.shape)
        )

    return sided


def line_kernel(up_ref, repair_ref, turn_ref):
    decay, _ = root_of(up_ref[pl.ds(ROWS, 8), :])
    whole = power_64(decay)
    around = whole
    for _ in range(4):
        around = around * around
    turn_ref[0] = whole
    turn_ref[1] = 1.0 / (1.0 - around)
    square = (CZ, CZ)
    y, side = flux_place(rows_of(square))
    low = side == 0
    base = sided_by(low)(decay[:1])
    place = lanes(square) == jnp.where(low, 0, CZ - 1)
    forth = jnp.where(place, raised(base, CY - 1 - y), 0.0)
    back = jnp.where(place, raised(base, y), 0.0)
    repair_ref[...] = paired(jnp.concatenate([forth, back], axis=1))


def line_matrices(up):
    shapes = [
        jax.ShapeDtypeStruct((2 * CZ, 4 * CZ), bf16),
        jax.ShapeDtypeStruct((2, 8, CZ), f32),
    ]
    return kernel_call(line_kernel, shapes, [VMEM] * 2, [VMEM], name="line_matrices")(up)


def repair_kernel(
    rank_ref, ends_ref, columns_ref, up_ref, low_ref, high_ref, repair_ref,
    out_ref, flux_ref, near_ref,
):
    rank = rank_ref[0]
    inner_low, inner_high = rank > 0, rank < NGZ - 1
    own, low_eta, high_eta = (ref[pl.ds(ROWS, 8), :] for ref in (up_ref, low_ref, high_ref))
    row = rows_of()
    near_ref[...] = jnp.where(row == 0, low_eta, jnp.where(row == 1, own, high_eta))
    own = own[:1]
    low_eta = jnp.where(inner_low, low_eta[:1], 0.0)[:, CZ - 1 :]
    high_eta = jnp.where(inner_high, high_eta[:1], 0.0)[:, :1]
    face_low = jnp.broadcast_to(z_rate * 0.5 * (low_eta + own[:, :1]), (1, CZ))
    face_high = jnp.broadcast_to(z_rate * 0.5 * (own[:, CZ - 1 :] + high_eta), (1, CZ))
    face = jnp.where(lanes((1, CZ)) & 1 == 0, face_low, face_high)
    face = jnp.broadcast_to(face, (ROWS, CZ))
    even = lanes((ROWS, CZ)) & 1 == 0
    low = jnp.where(inner_low, low_ref[:ROWS], 0.0)
    high = jnp.where(inner_high, high_ref[:ROWS], 0.0)
    outer = (
        jnp.where(even, pltpu.roll(low, 1, 1), pltpu.roll(high, 1, 1)),
        jnp.where(even, low, pltpu.roll(high, 2, 1)),
    )
    for half in range(2):
        at = pl.ds(half * ROWS, ROWS)
        columns = columns_ref[at, :]
        inner = jnp.where(even, columns, pltpu.roll(columns, 2, 1))
        flux = turned(face * (outer[half] - inner))
        flux_ref[at, :] = flux
        added = pair_dot(flux, repair_ref[...])
        out_ref[0, at, :] = ends_ref[0, at, :] + added[:, :CZ]
        out_ref[1, at, :] = ends_ref[1, at, :] + added[:, CZ:]


def repair(ranks, ends, columns, up, low, high, matrix):
    shapes = [
        jax.ShapeDtypeStruct((2, LINES, CZ), f32),
        FLAT,
        jax.ShapeDtypeStruct((NGZ, CZ), f32),
    ]
    call = kernel_call(repair_kernel, shapes, [VMEM] * 3, [SMEM] + [VMEM] * 6, name="repair")
    return call(ranks, ends, columns, up, low, high, matrix)


def ring_kernel(
    rank_ref, ends_ref, turn_ref, near_ref, far_low_ref, far_high_ref, out_ref, eta_ref, eta_buf
):
    eta_buf[0:2, :] = far_low_ref[1:3, :]
    eta_buf[2:5, :] = near_ref[0:3, :]
    eta_buf[5:8, :] = far_high_ref[0:3, :]
    eta_ref[...] = pltpu.roll(eta_buf[...], lax.rem(rank_ref[0] + 5, 8), 0)
    rows = 2 * LINES // NGY
    upward = rank_ref[1] < NGY // 2
    whole, closing = turn_ref[0], turn_ref[1]
    for part in range(rows // 8):

        def at(node):
            return pl.ds(node * rows + part * 8, 8)

        up = jnp.zeros((8, CZ), f32)
        down = jnp.zeros((8, CZ), f32)
        for node in range(NGY):
            up = up * whole + ends_ref[at(node), :]
            down = down * whole + ends_ref[at(NGY - 1 - node), :]
        up = up * closing
        down = down * closing
        ups, downs = [], [None] * NGY
        for node in range(NGY):
            ups.append(up)
            up = up * whole + ends_ref[at(node), :]
            downs[NGY - 1 - node] = down
            down = down * whole + ends_ref[at(NGY - 1 - node), :]
        for node in range(NGY):
            out_ref[at(node), :] = jnp.where(upward, ups[node], downs[node])


def ring_scan(ranks, ends, turn, near, far_low, far_high):
    rows = jax.ShapeDtypeStruct((NGZ, CZ), f32)
    return kernel_call(
        ring_kernel,
        [jax.ShapeDtypeStruct(ends.shape, f32), rows],
        [VMEM] * 2,
        [SMEM] + [VMEM] * 5,
        [pltpu.VMEM((NGZ, CZ), f32)],
        name="ring_scan",
    )(ranks, ends, turn, near, far_low, far_high)


def coefficient_kernel(
    rank_ref, eta_ref, table_ref, green_ref, ends_ref, carry_ref, share_ref, layer_ref, reach_ref,
):
    rank = rank_ref[0]
    lane, row = lanes(), rows_of()
    eta = eta_ref[...]

    def before(x, fill):
        y = pltpu.roll(x, 1, 1)
        return jnp.where(lane == 0, jnp.where(row == 0, fill, pltpu.roll(y, 1, 0)), y)

    def after(x, fill):
        y = pltpu.roll(x, CZ - 1, 1)
        edge = jnp.where(row == NGZ - 1, fill, pltpu.roll(y, NGZ - 1, 0))
        return jnp.where(lane == CZ - 1, edge, y)

    def last_of(x, end):
        return jnp.broadcast_to(x[:, end : end + 1], (8, CZ))

    face_low = z_rate * 0.5 * (before(eta, 0.0) + eta)
    face_high = z_rate * 0.5 * (eta + after(eta, 0.0))

    def pivots(face, up):
        scale = 1.0 / (1.0 + face)
        a = jnp.ones((8, CZ), f32)
        b = face * scale
        c = scale
        d = b
        step = 1
        while step < CZ:
            shift = step if up else CZ - step
            inside = lane >= step if up else lane < CZ - step
            pa, pb, pc, pd = (pltpu.roll(x, shift, 1) for x in (a, b, c, d))
            na, nb = a * pa + b * pc, a * pb + b * pd
            nc, nd = c * pa + d * pc, c * pb + d * pd
            a, b = jnp.where(inside, na, a), jnp.where(inside, nb, b)
            c, d = jnp.where(inside, nc, c), jnp.where(inside, nd, d)
            step *= 2
        end = CZ - 1 if up else 0
        ta, tb, tc, td = (last_of(x, end) for x in (a, b, c, d))
        edge = row == (0 if up else NGZ - 1)
        va, vc = jnp.ones((8, CZ), f32), jnp.zeros((8, CZ), f32)
        for _ in range(NGZ - 1):
            na, nc = ta * va + tb * vc, tc * va + td * vc
            size = 1.0 / (na + nc)
            shift = 1 if up else NGZ - 1
            va = jnp.where(edge, 1.0, pltpu.roll(na * size, shift, 0))
            vc = jnp.where(edge, 0.0, pltpu.roll(nc * size, shift, 0))
        return (a * va + b * vc) / (c * va + d * vc)

    delta_up = pivots(face_low, True)
    delta_down = pivots(face_high, False)
    inverse = 1.0 / (delta_up + delta_down - 1.0)
    first_cell = (lane == 0) & (row == 0)
    last_cell = (lane == CZ - 1) & (row == NGZ - 1)
    link_up = jnp.where(first_cell, 0.0, face_low / (face_low + before(delta_up, 1.0)))
    link_down = jnp.where(last_cell, 0.0, face_high / (face_high + after(delta_down, 1.0)))

    def running(x, up):
        step = 1
        while step < CZ:
            moved = pltpu.roll(x, step if up else CZ - step, 1)
            x = jnp.where(lane >= step if up else lane < CZ - step, x * moved, x)
            step *= 2
        return x

    product_up, product_down = running(link_up, True), running(link_down, False)
    across_up, across_down = last_of(product_up, CZ - 1), last_of(product_down, 0)
    share_up = jnp.zeros((8, CZ), f32)
    share_down = jnp.zeros((8, CZ), f32)
    for _ in range(NGZ - 1):
        moved = pltpu.roll(across_up * share_up, NGZ - 1, 0)
        share_up = jnp.where(row == rank - 1, 1.0, jnp.where(row < rank - 1, moved, 0.0))
        moved = pltpu.roll(across_down * share_down, 1, 0)
        share_down = jnp.where(row == rank + 1, 1.0, jnp.where(row > rank + 1, moved, 0.0))

    def own(x):
        return jnp.sum(jnp.where(row == rank, x, 0.0), axis=0, keepdims=True)

    scale = own(inverse)
    own_up, own_down = own(link_up), own(link_down)
    turned_by = lax.rem(NGZ - rank, NGZ)
    share_up = share_up * jnp.broadcast_to(own_up[:, :1], (8, CZ))
    share_down = share_down * jnp.broadcast_to(own_down[:, CZ - 1 :], (8, CZ))
    share_ref[0] = pltpu.roll(share_up, turned_by, 0)
    share_ref[1] = pltpu.roll(share_down, turned_by, 0)
    lane_1 = lanes((1, CZ))
    within_up = running(jnp.broadcast_to(jnp.where(lane_1 == 0, 1.0, own_up), (8, CZ)), True)
    within_down = running(
        jnp.broadcast_to(jnp.where(lane_1 == CZ - 1, 1.0, own_down), (8, CZ)), False
    )
    square = (CZ, CZ)
    lane_sq, row_sq = lanes(square), rows_of(square)
    carry = jnp.where(
        row_sq < CZ // 2,
        jnp.broadcast_to(within_up[:1] * scale, square),
        jnp.broadcast_to(within_down[:1] * scale, square),
    )
    identity = jnp.where(lane_sq == row_sq, 1.0, 0.0).astype(f32)

    def triangle(link, up):
        link = jnp.where(lanes((1, CZ)) == (0 if up else CZ - 1), 0.0, link)
        link = jnp.broadcast_to(link, (8, CZ))
        out = identity
        step = 1
        while step < CZ:
            shift = step if up else CZ - step
            out = out + jnp.broadcast_to(link[0:1, :], square) * pltpu.roll(out, shift, 1)
            link = link * pltpu.roll(link, shift, 1)
            step *= 2
        return out

    lower, upper = triangle(own_up, True), triangle(own_down, False)
    green = 2.0 * (lower + upper - identity) * jnp.broadcast_to(scale, square)
    ends = 2.0 * jnp.where(
        lane_sq < CZ // 2,
        jnp.broadcast_to(lower[:, CZ - 1 : CZ], square),
        jnp.broadcast_to(upper[:, 0:1], square),
    )
    for matrix, ref in ((green, green_ref), (ends, ends_ref), (carry, carry_ref)):
        ref[...] = paired(matrix)

    decay, peak = root_of(own(eta))
    y = row_sq & 63
    wide = jnp.broadcast_to(decay, square)
    start = jnp.broadcast_to(peak * decay, square)
    seen = jnp.transpose(ends)
    reach = []
    for way in range(2):
        response = start * raised(wide, (y, CY - 1 - y)[way])
        table_ref[way] = response[:CY]
        reach.append(jnp.transpose(response * seen))
    reach_ref[...] = paired(jnp.concatenate(reach, axis=0))
    y, side = flux_place(row_sq)
    low = side == 0
    sided = sided_by(low)
    base = sided(decay)
    apart = jnp.abs(y - (lane_sq & 63))
    spread = jnp.where(low == (lane_sq < 64), sided(peak) * raised(base, apart), 0.0)
    same_y = (lane_sq & 63) == (row_sq & 63)
    first = jnp.broadcast_to(ends[0:1, :], square)
    final = jnp.broadcast_to(ends[CZ - 1 :, :], square)
    layer = jnp.where(same_y, jnp.where(row_sq < 64, first, final), 0.0)
    layer_ref[...] = paired(jnp.concatenate([2.0 * spread, pair_dot(spread, paired(layer))], axis=1))


def coefficients(ranks, etas):
    def matrix(rows, columns):
        return jax.ShapeDtypeStruct((2 * rows * CZ, 2 * columns * CZ), bf16)

    return kernel_call(
        coefficient_kernel,
        [
            jax.ShapeDtypeStruct((2, CY, CZ), f32),
            matrix(1, 1),
            matrix(1, 1),
            matrix(1, 1),
            jax.ShapeDtypeStruct((2, NGZ, CZ), f32),
            matrix(1, 2),
            matrix(2, 1),
        ],
        [VMEM] * 7,
        [SMEM, VMEM],
        name="z_coefficients",
        us=4,
    )(ranks, etas)


def split_rows(left_ref, rows, x):
    high, mid = split(x)
    left_ref[rows, 0:CZ] = high
    left_ref[rows, CZ : 2 * CZ] = mid


def halves(result):
    return result[:, :CZ] + result[:, CZ:]


def fetches_of(u_hbm, m_hbm, u_ref, m_ref, sems):
    def fetches(i):
        return (
            pltpu.make_async_copy(pitched(m_hbm, i), pitched(m_ref, i), sems.at[0, i]),
            pltpu.make_async_copy(chunk(u_hbm, i), chunk(u_ref, i), sems.at[1, i]),
        )

    return fetches


def sums_kernel(
    m_hbm, u_hbm, ends_ref, flux_ref, spread_ref, sums_ref, layer_ref, m_ref, u_ref, left_ref, seen_ref, sems
):
    mask = unit_mask((CY, CZ))

    def prepare():
        both = pair_dot(flux_ref[...], spread_ref[...])
        layer_ref[...] = both[:, :CZ]
        seen_ref[...] = both[:, CZ:]

    def work(i):
        for g in range(PER // GROUP):
            left = left_ref.at[g % SLOTS]
            first = i * PER + g * GROUP
            for c in range(GROUP):
                line = first + c
                change = m_ref[pl.ds(line * PITCH, CY), :] - u_ref[line]
                split_rows(left, pl.ds(c * CY, CY), change)
            result = halves(jnp.dot(left[...], ends_ref[...], preferred_element_type=f32))
            for c in range(GROUP):
                part = jnp.where(mask, result[c * CY : (c + 1) * CY], 0.0)
                sums_ref[pl.ds(first + c, 1), :] = jnp.sum(part, axis=0, keepdims=True)

    pipeline(fetches_of(u_hbm, m_hbm, u_ref, m_ref, sems), no_copies, work, prepare)
    sums_ref[...] += seen_ref[...]


def local_sums(m, u, ends, flux, spread):
    return kernel_call(
        sums_kernel,
        [FLAT, FLAT],
        [VMEM] * 2,
        [HBM, HBM] + [VMEM] * 3,
        [
            pltpu.VMEM(PITCHED, f32),
            pltpu.VMEM((LINES, CY, CZ), f32),
            pltpu.VMEM((SLOTS, GROUP * CY, 2 * CZ), bf16),
            pltpu.VMEM((LINES, CZ), f32),
            pltpu.SemaphoreType.DMA((2, STEPS)),
        ],
        name="z_local_sums",
        mib=48,
        us=8,
    )(m, u, ends, flux, spread)


def messages_kernel(rank_ref, sums_ref, carry_ref, reach_ref, *out_refs):
    rank = rank_ref[0]
    carries = jnp.concatenate([carry_ref[0], carry_ref[1]], axis=1)
    sums = sums_ref[...] + pair_dot(carries, reach_ref[...])
    first, second = sums[:ROWS], sums[ROWS:]
    lower = lanes((ROWS, CZ)) < 64
    up = jnp.where(lower, first, pltpu.roll(second, 64, 1))
    down = jnp.where(lower, pltpu.roll(first, 64, 1), second)
    for k in range(1, NGZ):
        out_refs[k - 1][...] = jnp.where(rank >= k, down, up)


def messages_of(ranks, sums, carries, reach):
    shapes = [jax.ShapeDtypeStruct((ROWS, CZ), f32)] * (NGZ - 1)
    specs = [VMEM] * (NGZ - 1)
    call = kernel_call(messages_kernel, shapes, specs, [SMEM] + [VMEM] * 3, name="z_messages")
    return call(ranks, sums, carries, reach)


def solve_kernel(
    m_hbm, u_hbm, carry_ref, table_ref, green_ref, y_ref, m_ref, u_ref, left_ref, sems
):
    tall = (CY, CZ)

    def work(i):
        for g in range(PER // GROUP):
            left = left_ref.at[g % SLOTS]
            first = i * PER + g * GROUP
            for c in range(GROUP):
                line = first + c
                carry_up = jnp.broadcast_to(carry_ref[0, pl.ds(line, 1), :], tall)
                carry_down = jnp.broadcast_to(carry_ref[1, pl.ds(line, 1), :], tall)
                change = m_ref[pl.ds(line * PITCH, CY), :] - u_ref[line]
                change = change + table_ref[0] * carry_up + table_ref[1] * carry_down
                split_rows(left, pl.ds(c * CY, CY), change)
            result = halves(jnp.dot(left[...], green_ref[...], preferred_element_type=f32))
            for c in range(GROUP):
                y_ref[first + c] = u_ref[first + c] + result[c * CY : (c + 1) * CY]

    pipeline(fetches_of(u_hbm, m_hbm, u_ref, m_ref, sems), no_copies, work)


def local_solve(m, u, carries, table, green):
    return kernel_call(
        solve_kernel,
        CUBE,
        VMEM,
        [HBM, HBM] + [VMEM] * 3,
        [
            pltpu.VMEM(PITCHED, f32),
            pltpu.VMEM((LINES, CY, CZ), f32),
            pltpu.VMEM((SLOTS, GROUP * CY, 2 * CZ), bf16),
            pltpu.SemaphoreType.DMA((3, STEPS)),
        ],
        name="z_local_solve",
        mib=42,
        us=8,
    )(m, u, carries, table, green)


def finish_kernel(
    y_ref, matrix_ref, share_ref, layer_ref, *rest
):
    got_refs = rest[: NGZ - 1]
    out_hbm, out_ref, left_ref, high_ref, mid_ref, sems = rest[NGZ - 1 :]
    lower = lanes((ROWS, CZ)) < 64
    tall = (CY, CZ)
    mask = unit_mask(tall)

    def stores(i):
        return (pltpu.make_async_copy(chunk(out_ref, i), chunk(out_hbm, i), sems.at[1, i]),)

    def prepare():
        up = jnp.zeros((ROWS, CZ), f32)
        down = jnp.zeros((ROWS, CZ), f32)
        for k in range(1, NGZ):
            value = got_refs[k - 1][...]
            up += jnp.broadcast_to(share_ref[0, k : k + 1, :], (ROWS, CZ)) * value
            down += jnp.broadcast_to(share_ref[1, k : k + 1, :], (ROWS, CZ)) * value
        both = (
            jnp.where(lower, up, pltpu.roll(down, 64, 1)),
            jnp.where(lower, pltpu.roll(up, 64, 1), down),
        )
        for half in range(2):
            at = pl.ds(half * ROWS, ROWS)
            high, mid = split(both[half] + layer_ref[at, :])
            high_ref[at, :] = high.astype(f32)
            mid_ref[at, :] = mid.astype(f32)

    def work(i):
        for g in range(PER // GROUP):
            left = left_ref.at[g % SLOTS]
            first = i * PER + g * GROUP
            for c in range(GROUP):
                line = pl.ds(first + c, 1)
                at = pl.ds(c * CY, CY)
                high = jnp.broadcast_to(high_ref[line, :], tall)
                mid = jnp.broadcast_to(mid_ref[line, :], tall)
                left[at, 0:CZ] = jnp.where(mask, high, 0.0).astype(bf16)
                left[at, CZ:] = jnp.where(mask, mid, 0.0).astype(bf16)
            result = halves(jnp.dot(left[...], matrix_ref[...], preferred_element_type=f32))
            for c in range(GROUP):
                out_ref[first + c] = y_ref[first + c] + result[c * CY : (c + 1) * CY]

    pipeline(no_copies, stores, work, prepare)


def finish(y, matrix, share, layer, got):
    return kernel_call(
        finish_kernel,
        CUBE,
        HBM,
        [VMEM] * (NGZ + 3),
        [
            pltpu.VMEM((LINES, CY, CZ), f32),
            pltpu.VMEM((SLOTS, GROUP * CY, 2 * CZ), bf16),
            pltpu.VMEM((LINES, CZ), f32),
            pltpu.VMEM((LINES, CZ), f32),
            pltpu.SemaphoreType.DMA((2, STEPS)),
        ],
        name="z_carries",
        mib=42,
        us=8,
    )(y, matrix, share, layer, *got)


def shifted(x, axis, by):
    n = lax.axis_size(axis)
    return lax.ppermute(x, axis, [(i, (i + by) % n) for i in range(n)])


def body(fields, source_term, resistivity):
    u = fields.reshape(LINES, CY, CZ)
    q = source_term.reshape(LINES, CY, CZ)
    ranks = jnp.stack([lax.axis_index("gz"), lax.axis_index("gy")]).astype(jnp.int32)
    own = resistivity.reshape(1, CZ)
    m, ends, columns, up, down = sweeps(u, q, own)
    low, high = shifted(up, "gz", 1), shifted(down, "gz", -1)
    matrix, turn = line_matrices(up)
    ends, flux, near = repair(ranks, ends, columns, up, low, high, matrix)
    nodes = lax.all_to_all(ends.reshape(2 * LINES, CZ), "gy", 0, 0, tiled=True)
    far_low, far_high = shifted(near, "gz", 3), shifted(near, "gz", -3)
    nodes, etas = ring_scan(ranks, nodes, turn, near, far_low, far_high)
    carries = lax.all_to_all(nodes, "gy", 0, 0, tiled=True).reshape(2, LINES, CZ)
    table, green, last, vector, share, layers, reach = coefficients(ranks, etas)
    sums, layer = local_sums(m, u, last, flux, layers)
    messages = messages_of(ranks, sums, carries, reach)
    got = [shifted(x, "gz", -k) for k, x in enumerate(messages, start=1)]
    y = local_solve(m, u, carries, table, green)
    return finish(y, vector, share, layer, got).reshape(fields.shape)


def solution(mesh):
    return jax.shard_map(
        body,
        mesh=mesh,
        in_specs=(P(None, None, "gy", "gz"), P(None, None, "gy", "gz"), P("gz")),
        out_specs=P(None, None, "gy", "gz"),
        check_vma=False,
    )
```

```python
import jax
import jax.numpy as jnp
from jax import lax
from jax.experimental import pallas as pl
from jax.experimental.pallas import tpu as pltpu
from jax.sharding import PartitionSpec as P

f32 = jnp.float32
bf16 = jnp.bfloat16
z_rate = 1.0
y_rate = 0.25

LINES = 192
CY = 64
CZ = 128
GROUP = 8
PER = 32
STEPS = LINES // PER
BATCH = 16
SLOTS = 2
AHEAD = 6
PITCH = 65
NGY = 16
NGZ = 8


def lanes(shape=(8, CZ)):
    return lax.broadcasted_iota(jnp.int32, shape, len(shape) - 1)


def rows_of(shape=(8, CZ)):
    return lax.broadcasted_iota(jnp.int32, shape, 0)


def root_of(eta):
    k = y_rate * eta
    root = jnp.sqrt(1.0 + 4.0 * k)
    return 2.0 * k / (1.0 + 2.0 * k + root), 1.0 / root


def power_64(r):
    for _ in range(6):
        r = r * r
    return r


def split(x):
    high = x.astype(bf16)
    return high, (x - high.astype(f32)).astype(bf16)


def paired(x):
    high, mid = split(x)
    row = jnp.concatenate([high, mid], axis=1)
    return jnp.concatenate([row, row], axis=0)


def pair_dot(x, matrix):
    high, mid = split(x)
    result = jnp.dot(
        jnp.concatenate([high, mid], axis=1), matrix, preferred_element_type=f32
    )
    half = result.shape[1] // 2
    return result[:, :half] + result[:, half:]


def chunk(ref, step):
    return ref.at[pl.ds(step * PER, PER)]


def kernel_call(kernel, out_shape, out_specs, in_specs, scratch=(), name=None, us=1, mib=8):
    return pl.pallas_call(
        kernel,
        in_specs=in_specs,
        out_specs=out_specs,
        out_shape=out_shape,
        scratch_shapes=list(scratch),
        compiler_params=pltpu.CompilerParams(vmem_limit_bytes=mib * 1024 * 1024),
        cost_estimate=pl.CostEstimate(flops=0, bytes_accessed=us * 3_000_000, transcendentals=0),
        name=name,
    )


def pipeline(fetches, stores, work, prepare=None):
    for i in range(AHEAD):
        for copy in fetches(i):
            copy.start()
    if prepare:
        prepare()

    def step(i, _):
        @pl.when(i + AHEAD < STEPS)
        def _():
            for copy in fetches(i + AHEAD):
                copy.start()

        for copy in fetches(i):
            copy.wait()
        work(i)
        for copy in stores(i):
            copy.start()
        return 0

    lax.fori_loop(0, STEPS, step, 0)

    def drain(i, _):
        for copy in stores(i):
            copy.wait()
        return 0

    lax.fori_loop(0, STEPS, drain, 0)


def pitched(ref, step):
    start = step * PER * PITCH
    if not isinstance(step, int):
        start = pl.multiple_of(start, 8)
    return ref.at[pl.ds(start, PER * PITCH)]


def no_copies(i):
    return ()


def unit_mask(tall):
    return (lanes(tall) & 63) == rows_of(tall)


VMEM = pl.BlockSpec(memory_space=pltpu.VMEM)
SMEM = pl.BlockSpec(memory_space=pltpu.SMEM)
HBM = pl.BlockSpec(memory_space=pltpu.HBM)
CUBE = jax.ShapeDtypeStruct((LINES, CY, CZ), f32)
FLAT = jax.ShapeDtypeStruct((LINES, CZ), f32)
PITCHED = (LINES * PITCH, CZ)
ROWS = LINES // 2
HALO = jax.ShapeDtypeStruct((ROWS + 8, CZ), f32)


def sweep_kernel(
    u_hbm, q_hbm, eta_hbm, m_hbm, ends_ref, columns_ref, up_ref, down_ref,
    u_ref, q_ref, m_ref, x_buf, f_buf, eta_ref, eta_sem, sems,
):
    lane = lanes()
    place = ((lane + 1) >> 1) & 63

    def fetches(i):
        return (
            pltpu.make_async_copy(chunk(u_hbm, i), chunk(u_ref, i), sems.at[0, i]),
            pltpu.make_async_copy(chunk(q_hbm, i), chunk(q_ref, i), sems.at[1, i]),
        )

    def stores(i):
        return (pltpu.make_async_copy(pitched(m_ref, i), pitched(m_hbm, i), sems.at[2, i]),)

    eta_copy = pltpu.make_async_copy(eta_hbm, eta_ref, eta_sem)
    eta_copy.start()
    for i in range(AHEAD):
        for copy in fetches(i):
            copy.start()
    eta_copy.wait()
    eta = jnp.broadcast_to(eta_ref[...], (8, CZ))
    up_ref[pl.ds(ROWS, 8), :] = eta
    down_ref[pl.ds(ROWS, 8), :] = eta
    face_low = jnp.where(lane == 0, 0.0, z_rate * 0.5 * (pltpu.roll(eta, 1, 1) + eta))
    face_high = jnp.where(lane == CZ - 1, 0.0, z_rate * 0.5 * (eta + pltpu.roll(eta, CZ - 1, 1)))
    decay, peak = root_of(eta)
    groups = PER // GROUP

    size = PER * PITCH
    half = CY // 2

    def rows(i, g):
        return pl.ds(pl.multiple_of(i * PER + g * GROUP, 8), GROUP)

    def right_side(i, tiles, acc):
        for tile in tiles:
            g, k = tile // 64, tile % 64
            c, at = tile // 8, pl.ds((tile % 8) * 8, 8)
            here = u_ref[i * PER + c, at, :]
            under = pltpu.roll(here, 1, 1)
            over = pltpu.roll(here, CZ - 1, 1)
            acc = jnp.where(place == k, pltpu.roll(here, 2 * k, 1) if k else here, acc)
            q = q_ref[i * PER + c, at, :].astype(f32)
            explicit = face_high * (over - here) - face_low * (here - under)
            x_buf[pl.ds((i % 2) * size + c * PITCH + (tile % 8) * 8, 8), :] = here + explicit + q
            if k == 63:
                columns_ref[rows(i, g), :] = acc
        return acc

    def sweep(i, ahead):
        def x_at(g, y):
            return x_buf[pl.ds((i % 2) * size + g * GROUP * PITCH + y, GROUP, stride=PITCH), :]

        def at(g, y):
            return pl.ds(g * GROUP * PITCH + y, GROUP, stride=PITCH)

        def out(g, y):
            return pl.ds(i * size + g * GROUP * PITCH + y, GROUP, stride=PITCH)

        acc = jnp.zeros((8, CZ), f32)
        forth = [acc] * groups
        back = [acc] * groups
        for s in range(CY):
            low, high = s, CY - 1 - s
            for g in range(groups):
                forth[g] = forth[g] * decay + x_at(g, low)
                kept = back[g] * decay
                back[g] = kept + x_at(g, high)
                if s < half:
                    f_buf[at(g, low), :] = forth[g]
                    f_buf[at(g, high), :] = kept
                else:
                    m_ref[out(g, low), :] = peak * (forth[g] + f_buf[at(g, low), :])
                    m_ref[out(g, high), :] = peak * (f_buf[at(g, high), :] + kept)
            if ahead:
                each = PER * CY // 8 // CY
                acc = right_side(i + 1, range(s * each, (s + 1) * each), acc)
        for g in range(groups):
            ends_ref[0, rows(i, g), :] = forth[g]
            ends_ref[1, rows(i, g), :] = back[g]

    for copy in fetches(0):
        copy.wait()
    right_side(0, range(PER * CY // 8), jnp.zeros((8, CZ), f32))

    def step(i, _):
        @pl.when(i + AHEAD < STEPS)
        def _():
            for copy in fetches(i + AHEAD):
                copy.start()

        for copy in fetches(i + 1):
            copy.wait()
        sweep(i, True)
        for copy in stores(i):
            copy.start()
        return 0

    lax.fori_loop(0, STEPS - 1, step, 0)
    sweep(STEPS - 1, False)
    for copy in stores(STEPS - 1):
        copy.start()
    for i in range(STEPS):
        for copy in stores(i):
            copy.wait()
    first, second = columns_ref[:ROWS], columns_ref[ROWS:]
    odd = lanes((ROWS, CZ)) & 1 == 1
    up_ref[:ROWS] = jnp.where(odd, first, pltpu.roll(second, 1, 1))
    down_ref[:ROWS] = jnp.where(odd, pltpu.roll(second, CZ - 1, 1), first)


def sweeps(u, q, own):
    return kernel_call(
        sweep_kernel,
        [
            jax.ShapeDtypeStruct(PITCHED, f32),
            jax.ShapeDtypeStruct((2, LINES, CZ), f32),
            FLAT,
            HALO,
            HALO,
        ],
        [HBM] + [VMEM] * 4,
        [HBM] * 3,
        [
            pltpu.VMEM((LINES, CY, CZ), f32),
            pltpu.VMEM((LINES, CY, CZ), bf16),
            pltpu.VMEM(PITCHED, f32),
            pltpu.VMEM((2 * PER * PITCH, CZ), f32),
            pltpu.VMEM((PER * PITCH, CZ), f32),
            pltpu.VMEM((1, CZ), f32),
            pltpu.SemaphoreType.DMA,
            pltpu.SemaphoreType.DMA((3, STEPS)),
        ],
        name="y_sweeps",
        mib=51,
        us=12,
    )(u, q, own)


def raised(base, exponent, bits=6):
    out = jnp.ones_like(base)
    for bit in range(bits):
        out = jnp.where((exponent >> bit) & 1 == 1, out * base, out)
        base = base * base
    return out


def flux_place(l):
    return 8 * ((l >> 1) & 7) + (l >> 4), l & 1


def turned(x):
    lane, row = lanes(x.shape), rows_of(x.shape)
    for bit in range(3):
        rows, columns = 1 << bit, 16 << bit
        in_row, in_lane = (row >> bit) & 1, (lane >> (4 + bit)) & 1
        count = x.shape[0]
        forth = pltpu.roll(pltpu.roll(x, count - rows, 0), columns, 1)
        back = pltpu.roll(pltpu.roll(x, rows, 0), CZ - columns, 1)
        x = jnp.where(in_row == in_lane, x, jnp.where(in_row == 0, forth, back))
    return x


def sided_by(low):
    def sided(x):
        return jnp.where(
            low, jnp.broadcast_to(x[:, :1], low.shape), jnp.broadcast_to(x[:, CZ - 1 :], low.shape)
        )

    return sided


def line_kernel(up_ref, repair_ref, turn_ref):
    decay, _ = root_of(up_ref[pl.ds(ROWS, 8), :])
    whole = power_64(decay)
    around = whole
    for _ in range(4):
        around = around * around
    turn_ref[0] = whole
    turn_ref[1] = 1.0 / (1.0 - around)
    square = (CZ, CZ)
    y, side = flux_place(rows_of(square))
    low = side == 0
    base = sided_by(low)(decay[:1])
    place = lanes(square) == jnp.where(low, 0, CZ - 1)
    forth = jnp.where(place, raised(base, CY - 1 - y), 0.0)
    back = jnp.where(place, raised(base, y), 0.0)
    repair_ref[...] = paired(jnp.concatenate([forth, back], axis=1))


def line_matrices(up):
    shapes = [
        jax.ShapeDtypeStruct((2 * CZ, 4 * CZ), bf16),
        jax.ShapeDtypeStruct((2, 8, CZ), f32),
    ]
    return kernel_call(line_kernel, shapes, [VMEM] * 2, [VMEM], name="line_matrices")(up)


def repair_kernel(
    rank_ref, ends_ref, columns_ref, up_ref, low_ref, high_ref, repair_ref,
    out_ref, flux_ref, near_ref,
):
    rank = rank_ref[0]
    inner_low, inner_high = rank > 0, rank < NGZ - 1
    own, low_eta, high_eta = (ref[pl.ds(ROWS, 8), :] for ref in (up_ref, low_ref, high_ref))
    row = rows_of()
    near_ref[...] = jnp.where(row == 0, low_eta, jnp.where(row == 1, own, high_eta))
    own = own[:1]
    low_eta = jnp.where(inner_low, low_eta[:1], 0.0)[:, CZ - 1 :]
    high_eta = jnp.where(inner_high, high_eta[:1], 0.0)[:, :1]
    face_low = jnp.broadcast_to(z_rate * 0.5 * (low_eta + own[:, :1]), (1, CZ))
    face_high = jnp.broadcast_to(z_rate * 0.5 * (own[:, CZ - 1 :] + high_eta), (1, CZ))
    face = jnp.where(lanes((1, CZ)) & 1 == 0, face_low, face_high)
    face = jnp.broadcast_to(face, (ROWS, CZ))
    even = lanes((ROWS, CZ)) & 1 == 0
    low = jnp.where(inner_low, low_ref[:ROWS], 0.0)
    high = jnp.where(inner_high, high_ref[:ROWS], 0.0)
    outer = (
        jnp.where(even, pltpu.roll(low, 1, 1), pltpu.roll(high, 1, 1)),
        jnp.where(even, low, pltpu.roll(high, 2, 1)),
    )
    for half in range(2):
        at = pl.ds(half * ROWS, ROWS)
        columns = columns_ref[at, :]
        inner = jnp.where(even, columns, pltpu.roll(columns, 2, 1))
        flux = turned(face * (outer[half] - inner))
        flux_ref[at, :] = flux
        added = pair_dot(flux, repair_ref[...])
        out_ref[0, at, :] = ends_ref[0, at, :] + added[:, :CZ]
        out_ref[1, at, :] = ends_ref[1, at, :] + added[:, CZ:]


def repair(ranks, ends, columns, up, low, high, matrix):
    shapes = [
        jax.ShapeDtypeStruct((2, LINES, CZ), f32),
        FLAT,
        jax.ShapeDtypeStruct((NGZ, CZ), f32),
    ]
    call = kernel_call(repair_kernel, shapes, [VMEM] * 3, [SMEM] + [VMEM] * 6, name="repair")
    return call(ranks, ends, columns, up, low, high, matrix)


def ring_kernel(
    rank_ref, ends_ref, turn_ref, near_ref, far_low_ref, far_high_ref, out_ref, eta_ref, eta_buf
):
    eta_buf[0:2, :] = far_low_ref[1:3, :]
    eta_buf[2:5, :] = near_ref[0:3, :]
    eta_buf[5:8, :] = far_high_ref[0:3, :]
    eta_ref[...] = pltpu.roll(eta_buf[...], lax.rem(rank_ref[0] + 5, 8), 0)
    rows = 2 * LINES // NGY
    upward = rank_ref[1] < NGY // 2
    whole, closing = turn_ref[0], turn_ref[1]
    for part in range(rows // 8):

        def at(node):
            return pl.ds(node * rows + part * 8, 8)

        up = jnp.zeros((8, CZ), f32)
        down = jnp.zeros((8, CZ), f32)
        for node in range(NGY):
            up = up * whole + ends_ref[at(node), :]
            down = down * whole + ends_ref[at(NGY - 1 - node), :]
        up = up * closing
        down = down * closing
        ups, downs = [], [None] * NGY
        for node in range(NGY):
            ups.append(up)
            up = up * whole + ends_ref[at(node), :]
            downs[NGY - 1 - node] = down
            down = down * whole + ends_ref[at(NGY - 1 - node), :]
        for node in range(NGY):
            out_ref[at(node), :] = jnp.where(upward, ups[node], downs[node])


def ring_scan(ranks, ends, turn, near, far_low, far_high):
    rows = jax.ShapeDtypeStruct((NGZ, CZ), f32)
    return kernel_call(
        ring_kernel,
        [jax.ShapeDtypeStruct(ends.shape, f32), rows],
        [VMEM] * 2,
        [SMEM] + [VMEM] * 5,
        [pltpu.VMEM((NGZ, CZ), f32)],
        name="ring_scan",
    )(ranks, ends, turn, near, far_low, far_high)


def coefficient_kernel(
    rank_ref, eta_ref, table_ref, green_ref, ends_ref, carry_ref, share_ref, layer_ref, reach_ref,
):
    rank = rank_ref[0]
    lane, row = lanes(), rows_of()
    eta = eta_ref[...]

    def before(x, fill):
        y = pltpu.roll(x, 1, 1)
        return jnp.where(lane == 0, jnp.where(row == 0, fill, pltpu.roll(y, 1, 0)), y)

    def after(x, fill):
        y = pltpu.roll(x, CZ - 1, 1)
        edge = jnp.where(row == NGZ - 1, fill, pltpu.roll(y, NGZ - 1, 0))
        return jnp.where(lane == CZ - 1, edge, y)

    def last_of(x, end):
        return jnp.broadcast_to(x[:, end : end + 1], (8, CZ))

    face_low = z_rate * 0.5 * (before(eta, 0.0) + eta)
    face_high = z_rate * 0.5 * (eta + after(eta, 0.0))

    def pivots(face, up):
        scale = 1.0 / (1.0 + face)
        a = jnp.ones((8, CZ), f32)
        b = face * scale
        c = scale
        d = b
        step = 1
        while step < CZ:
            shift = step if up else CZ - step
            inside = lane >= step if up else lane < CZ - step
            pa, pb, pc, pd = (pltpu.roll(x, shift, 1) for x in (a, b, c, d))
            na, nb = a * pa + b * pc, a * pb + b * pd
            nc, nd = c * pa + d * pc, c * pb + d * pd
            a, b = jnp.where(inside, na, a), jnp.where(inside, nb, b)
            c, d = jnp.where(inside, nc, c), jnp.where(inside, nd, d)
            step *= 2
        end = CZ - 1 if up else 0
        ta, tb, tc, td = (last_of(x, end) for x in (a, b, c, d))
        edge = row == (0 if up else NGZ - 1)
        va, vc = jnp.ones((8, CZ), f32), jnp.zeros((8, CZ), f32)
        for _ in range(NGZ - 1):
            na, nc = ta * va + tb * vc, tc * va + td * vc
            size = 1.0 / (na + nc)
            shift = 1 if up else NGZ - 1
            va = jnp.where(edge, 1.0, pltpu.roll(na * size, shift, 0))
            vc = jnp.where(edge, 0.0, pltpu.roll(nc * size, shift, 0))
        return (a * va + b * vc) / (c * va + d * vc)

    delta_up = pivots(face_low, True)
    delta_down = pivots(face_high, False)
    inverse = 1.0 / (delta_up + delta_down - 1.0)
    first_cell = (lane == 0) & (row == 0)
    last_cell = (lane == CZ - 1) & (row == NGZ - 1)
    link_up = jnp.where(first_cell, 0.0, face_low / (face_low + before(delta_up, 1.0)))
    link_down = jnp.where(last_cell, 0.0, face_high / (face_high + after(delta_down, 1.0)))

    def running(x, up):
        step = 1
        while step < CZ:
            moved = pltpu.roll(x, step if up else CZ - step, 1)
            x = jnp.where(lane >= step if up else lane < CZ - step, x * moved, x)
            step *= 2
        return x

    product_up, product_down = running(link_up, True), running(link_down, False)
    across_up, across_down = last_of(product_up, CZ - 1), last_of(product_down, 0)
    share_up = jnp.zeros((8, CZ), f32)
    share_down = jnp.zeros((8, CZ), f32)
    for _ in range(NGZ - 1):
        moved = pltpu.roll(across_up * share_up, NGZ - 1, 0)
        share_up = jnp.where(row == rank - 1, 1.0, jnp.where(row < rank - 1, moved, 0.0))
        moved = pltpu.roll(across_down * share_down, 1, 0)
        share_down = jnp.where(row == rank + 1, 1.0, jnp.where(row > rank + 1, moved, 0.0))

    def own(x):
        return jnp.sum(jnp.where(row == rank, x, 0.0), axis=0, keepdims=True)

    scale = own(inverse)
    own_up, own_down = own(link_up), own(link_down)
    turned_by = lax.rem(NGZ - rank, NGZ)
    share_up = share_up * jnp.broadcast_to(own_up[:, :1], (8, CZ))
    share_down = share_down * jnp.broadcast_to(own_down[:, CZ - 1 :], (8, CZ))
    share_ref[0] = pltpu.roll(share_up, turned_by, 0)
    share_ref[1] = pltpu.roll(share_down, turned_by, 0)
    lane_1 = lanes((1, CZ))
    within_up = running(jnp.broadcast_to(jnp.where(lane_1 == 0, 1.0, own_up), (8, CZ)), True)
    within_down = running(
        jnp.broadcast_to(jnp.where(lane_1 == CZ - 1, 1.0, own_down), (8, CZ)), False
    )
    square = (CZ, CZ)
    lane_sq, row_sq = lanes(square), rows_of(square)
    carry = jnp.where(
        row_sq < CZ // 2,
        jnp.broadcast_to(within_up[:1] * scale, square),
        jnp.broadcast_to(within_down[:1] * scale, square),
    )
    identity = jnp.where(lane_sq == row_sq, 1.0, 0.0).astype(f32)

    def triangle(link, up):
        link = jnp.where(lanes((1, CZ)) == (0 if up else CZ - 1), 0.0, link)
        link = jnp.broadcast_to(link, (8, CZ))
        out = identity
        step = 1
        while step < CZ:
            shift = step if up else CZ - step
            out = out + jnp.broadcast_to(link[0:1, :], square) * pltpu.roll(out, shift, 1)
            link = link * pltpu.roll(link, shift, 1)
            step *= 2
        return out

    lower, upper = triangle(own_up, True), triangle(own_down, False)
    green = 2.0 * (lower + upper - identity) * jnp.broadcast_to(scale, square)
    ends = 2.0 * jnp.where(
        lane_sq < CZ // 2,
        jnp.broadcast_to(lower[:, CZ - 1 : CZ], square),
        jnp.broadcast_to(upper[:, 0:1], square),
    )
    for matrix, ref in ((green, green_ref), (ends, ends_ref), (carry, carry_ref)):
        ref[...] = paired(matrix)

    decay, peak = root_of(own(eta))
    y = row_sq & 63
    wide = jnp.broadcast_to(decay, square)
    start = jnp.broadcast_to(peak * decay, square)
    seen = jnp.transpose(ends)
    reach = []
    for way in range(2):
        response = start * raised(wide, (y, CY - 1 - y)[way])
        table_ref[way] = response[:CY]
        reach.append(jnp.transpose(response * seen))
    reach_ref[...] = paired(jnp.concatenate(reach, axis=0))
    y, side = flux_place(row_sq)
    low = side == 0
    sided = sided_by(low)
    base = sided(decay)
    apart = jnp.abs(y - (lane_sq & 63))
    spread = jnp.where(low == (lane_sq < 64), sided(peak) * raised(base, apart), 0.0)
    same_y = (lane_sq & 63) == (row_sq & 63)
    first = jnp.broadcast_to(ends[0:1, :], square)
    final = jnp.broadcast_to(ends[CZ - 1 :, :], square)
    layer = jnp.where(same_y, jnp.where(row_sq < 64, first, final), 0.0)
    layer_ref[...] = paired(jnp.concatenate([2.0 * spread, pair_dot(spread, paired(layer))], axis=1))


def coefficients(ranks, etas):
    def matrix(rows, columns):
        return jax.ShapeDtypeStruct((2 * rows * CZ, 2 * columns * CZ), bf16)

    return kernel_call(
        coefficient_kernel,
        [
            jax.ShapeDtypeStruct((2, CY, CZ), f32),
            matrix(1, 1),
            matrix(1, 1),
            matrix(1, 1),
            jax.ShapeDtypeStruct((2, NGZ, CZ), f32),
            matrix(1, 2),
            matrix(2, 1),
        ],
        [VMEM] * 7,
        [SMEM, VMEM],
        name="z_coefficients",
        us=4,
    )(ranks, etas)


def split_rows(left_ref, rows, x):
    high, mid = split(x)
    left_ref[rows, 0:CZ] = high
    left_ref[rows, CZ : 2 * CZ] = mid


def halves(result):
    return result[:, :CZ] + result[:, CZ:]


def fetches_of(u_hbm, m_hbm, u_ref, m_ref, sems):
    def fetches(i):
        return (
            pltpu.make_async_copy(pitched(m_hbm, i), pitched(m_ref, i), sems.at[0, i]),
            pltpu.make_async_copy(chunk(u_hbm, i), chunk(u_ref, i), sems.at[1, i]),
        )

    return fetches


def sums_kernel(
    m_hbm, u_hbm, ends_ref, flux_ref, spread_ref, sums_ref, layer_ref, m_ref, u_ref, left_ref, seen_ref, sems
):
    mask = unit_mask((CY, CZ))

    def prepare():
        both = pair_dot(flux_ref[...], spread_ref[...])
        layer_ref[...] = both[:, :CZ]
        seen_ref[...] = both[:, CZ:]

    def work(i):
        near_m = pitched(m_ref, i)
        for g in range(PER // BATCH):
            left = left_ref.at[g % SLOTS]
            first = i * PER + g * BATCH
            for c in range(BATCH):
                line = first + c
                change = near_m[pl.ds((g * BATCH + c) * PITCH, CY), :] - u_ref[line]
                split_rows(left, pl.ds(c * CY, CY), change)
            result = halves(jnp.dot(left[...], ends_ref[...], preferred_element_type=f32))
            for c in range(BATCH):
                part = jnp.where(mask, result[c * CY : (c + 1) * CY], 0.0)
                sums_ref[pl.ds(first + c, 1), :] = jnp.sum(part, axis=0, keepdims=True)

    pipeline(fetches_of(u_hbm, m_hbm, u_ref, m_ref, sems), no_copies, work, prepare)
    sums_ref[...] += seen_ref[...]


def local_sums(m, u, ends, flux, spread):
    return kernel_call(
        sums_kernel,
        [FLAT, FLAT],
        [VMEM] * 2,
        [HBM, HBM] + [VMEM] * 3,
        [
            pltpu.VMEM(PITCHED, f32),
            pltpu.VMEM((LINES, CY, CZ), f32),
            pltpu.VMEM((SLOTS, BATCH * CY, 2 * CZ), bf16),
            pltpu.VMEM((LINES, CZ), f32),
            pltpu.SemaphoreType.DMA((2, STEPS)),
        ],
        name="z_local_sums",
        mib=48,
        us=8,
    )(m, u, ends, flux, spread)


def messages_kernel(rank_ref, sums_ref, carry_ref, reach_ref, *out_refs):
    rank = rank_ref[0]
    carries = jnp.concatenate([carry_ref[0], carry_ref[1]], axis=1)
    sums = sums_ref[...] + pair_dot(carries, reach_ref[...])
    first, second = sums[:ROWS], sums[ROWS:]
    lower = lanes((ROWS, CZ)) < 64
    up = jnp.where(lower, first, pltpu.roll(second, 64, 1))
    down = jnp.where(lower, pltpu.roll(first, 64, 1), second)
    for k in range(1, NGZ):
        out_refs[k - 1][...] = jnp.where(rank >= k, down, up)


def messages_of(ranks, sums, carries, reach):
    shapes = [jax.ShapeDtypeStruct((ROWS, CZ), f32)] * (NGZ - 1)
    specs = [VMEM] * (NGZ - 1)
    call = kernel_call(messages_kernel, shapes, specs, [SMEM] + [VMEM] * 3, name="z_messages")
    return call(ranks, sums, carries, reach)


def solve_kernel(
    m_hbm, u_hbm, carry_ref, table_ref, green_ref, y_ref, m_ref, u_ref, left_ref, sems
):
    tall = (CY, CZ)

    def work(i):
        near_m = pitched(m_ref, i)
        for g in range(PER // BATCH):
            left = left_ref.at[g % SLOTS]
            first = i * PER + g * BATCH
            for c in range(BATCH):
                line = first + c
                carry_up = jnp.broadcast_to(carry_ref[0, pl.ds(line, 1), :], tall)
                carry_down = jnp.broadcast_to(carry_ref[1, pl.ds(line, 1), :], tall)
                change = near_m[pl.ds((g * BATCH + c) * PITCH, CY), :] - u_ref[line]
                change = change + table_ref[0] * carry_up + table_ref[1] * carry_down
                split_rows(left, pl.ds(c * CY, CY), change)
            result = halves(jnp.dot(left[...], green_ref[...], preferred_element_type=f32))
            for c in range(BATCH):
                y_ref[first + c] = u_ref[first + c] + result[c * CY : (c + 1) * CY]

    pipeline(fetches_of(u_hbm, m_hbm, u_ref, m_ref, sems), no_copies, work)


def local_solve(m, u, carries, table, green):
    return kernel_call(
        solve_kernel,
        CUBE,
        VMEM,
        [HBM, HBM] + [VMEM] * 3,
        [
            pltpu.VMEM(PITCHED, f32),
            pltpu.VMEM((LINES, CY, CZ), f32),
            pltpu.VMEM((SLOTS, BATCH * CY, 2 * CZ), bf16),
            pltpu.SemaphoreType.DMA((3, STEPS)),
        ],
        name="z_local_solve",
        mib=42,
        us=8,
    )(m, u, carries, table, green)


def finish_kernel(
    y_ref, matrix_ref, share_ref, layer_ref, *rest
):
    got_refs = rest[: NGZ - 1]
    out_hbm, out_ref, left_ref, high_ref, mid_ref, sems = rest[NGZ - 1 :]
    lower = lanes((ROWS, CZ)) < 64
    tall = (CY, CZ)
    mask = unit_mask(tall)

    def stores(i):
        return (pltpu.make_async_copy(chunk(out_ref, i), chunk(out_hbm, i), sems.at[1, i]),)

    def prepare():
        up = jnp.zeros((ROWS, CZ), f32)
        down = jnp.zeros((ROWS, CZ), f32)
        for k in range(1, NGZ):
            value = got_refs[k - 1][...]
            up += jnp.broadcast_to(share_ref[0, k : k + 1, :], (ROWS, CZ)) * value
            down += jnp.broadcast_to(share_ref[1, k : k + 1, :], (ROWS, CZ)) * value
        both = (
            jnp.where(lower, up, pltpu.roll(down, 64, 1)),
            jnp.where(lower, pltpu.roll(up, 64, 1), down),
        )
        for half in range(2):
            at = pl.ds(half * ROWS, ROWS)
            high, mid = split(both[half] + layer_ref[at, :])
            high_ref[at, :] = high.astype(f32)
            mid_ref[at, :] = mid.astype(f32)

    def work(i):
        for g in range(PER // BATCH):
            left = left_ref.at[g % SLOTS]
            first = i * PER + g * BATCH
            for c in range(BATCH):
                line = pl.ds(first + c, 1)
                at = pl.ds(c * CY, CY)
                high = jnp.broadcast_to(high_ref[line, :], tall)
                mid = jnp.broadcast_to(mid_ref[line, :], tall)
                left[at, 0:CZ] = jnp.where(mask, high, 0.0).astype(bf16)
                left[at, CZ:] = jnp.where(mask, mid, 0.0).astype(bf16)
            result = halves(jnp.dot(left[...], matrix_ref[...], preferred_element_type=f32))
            for c in range(BATCH):
                out_ref[first + c] = y_ref[first + c] + result[c * CY : (c + 1) * CY]

    pipeline(no_copies, stores, work, prepare)


def finish(y, matrix, share, layer, got):
    return kernel_call(
        finish_kernel,
        CUBE,
        HBM,
        [VMEM] * (NGZ + 3),
        [
            pltpu.VMEM((LINES, CY, CZ), f32),
            pltpu.VMEM((SLOTS, BATCH * CY, 2 * CZ), bf16),
            pltpu.VMEM((LINES, CZ), f32),
            pltpu.VMEM((LINES, CZ), f32),
            pltpu.SemaphoreType.DMA((2, STEPS)),
        ],
        name="z_carries",
        mib=42,
        us=8,
    )(y, matrix, share, layer, *got)


def shifted(x, axis, by):
    n = lax.axis_size(axis)
    return lax.ppermute(x, axis, [(i, (i + by) % n) for i in range(n)])


def body(fields, source_term, resistivity):
    u = fields.reshape(LINES, CY, CZ)
    q = source_term.reshape(LINES, CY, CZ)
    ranks = jnp.stack([lax.axis_index("gz"), lax.axis_index("gy")]).astype(jnp.int32)
    own = resistivity.reshape(1, CZ)
    m, ends, columns, up, down = sweeps(u, q, own)
    low, high = shifted(up, "gz", 1), shifted(down, "gz", -1)
    matrix, turn = line_matrices(up)
    ends, flux, near = repair(ranks, ends, columns, up, low, high, matrix)
    nodes = lax.all_to_all(ends.reshape(2 * LINES, CZ), "gy", 0, 0, tiled=True)
    far_low, far_high = shifted(near, "gz", 3), shifted(near, "gz", -3)
    nodes, etas = ring_scan(ranks, nodes, turn, near, far_low, far_high)
    carries = lax.all_to_all(nodes, "gy", 0, 0, tiled=True).reshape(2, LINES, CZ)
    table, green, last, vector, share, layers, reach = coefficients(ranks, etas)
    sums, layer = local_sums(m, u, last, flux, layers)
    messages = messages_of(ranks, sums, carries, reach)
    got = [shifted(x, "gz", -k) for k, x in enumerate(messages, start=1)]
    y = local_solve(m, u, carries, table, green)
    return finish(y, vector, share, layer, got).reshape(fields.shape)


def solution(mesh):
    return jax.shard_map(
        body,
        mesh=mesh,
        in_specs=(P(None, None, "gy", "gz"), P(None, None, "gy", "gz"), P("gz")),
        out_specs=P(None, None, "gy", "gz"),
        check_vma=False,
    )
```

```python
import jax
import jax.numpy as jnp
from jax import lax
from jax.experimental import pallas as pl
from jax.experimental.pallas import tpu as pltpu
from jax.sharding import PartitionSpec as P

f32 = jnp.float32
bf16 = jnp.bfloat16
z_rate = 1.0
y_rate = 0.25

LINES = 192
CY = 64
CZ = 128
GROUP = 8
PER = 32
STEPS = LINES // PER
BATCH = 16
SLOTS = 2
AHEAD = 6
PITCH = 65
NGY = 16
NGZ = 8


def lanes(shape=(8, CZ)):
    return lax.broadcasted_iota(jnp.int32, shape, len(shape) - 1)


def rows_of(shape=(8, CZ)):
    return lax.broadcasted_iota(jnp.int32, shape, 0)


def root_of(eta):
    k = y_rate * eta
    root = jnp.sqrt(1.0 + 4.0 * k)
    return 2.0 * k / (1.0 + 2.0 * k + root), 1.0 / root


def power_64(r):
    for _ in range(6):
        r = r * r
    return r


def split(x):
    high = x.astype(bf16)
    return high, (x - high.astype(f32)).astype(bf16)


def paired(x):
    high, mid = split(x)
    row = jnp.concatenate([high, mid], axis=1)
    return jnp.concatenate([row, row], axis=0)


def pair_dot(x, matrix):
    high, mid = split(x)
    result = jnp.dot(
        jnp.concatenate([high, mid], axis=1), matrix, preferred_element_type=f32
    )
    half = result.shape[1] // 2
    return result[:, :half] + result[:, half:]


def chunk(ref, step):
    return ref.at[pl.ds(step * PER, PER)]


def kernel_call(kernel, out_shape, out_specs, in_specs, scratch=(), name=None, us=1, mib=8):
    return pl.pallas_call(
        kernel,
        in_specs=in_specs,
        out_specs=out_specs,
        out_shape=out_shape,
        scratch_shapes=list(scratch),
        compiler_params=pltpu.CompilerParams(vmem_limit_bytes=mib * 1024 * 1024),
        cost_estimate=pl.CostEstimate(flops=0, bytes_accessed=us * 3_000_000, transcendentals=0),
        name=name,
    )


def pipeline(fetches, stores, work, prepare=None):
    for i in range(AHEAD):
        for copy in fetches(i):
            copy.start()
    if prepare:
        prepare()

    def step(i, _):
        @pl.when(i + AHEAD < STEPS)
        def _():
            for copy in fetches(i + AHEAD):
                copy.start()

        for copy in fetches(i):
            copy.wait()
        work(i)
        for copy in stores(i):
            copy.start()
        return 0

    lax.fori_loop(0, STEPS, step, 0)

    def drain(i, _):
        for copy in stores(i):
            copy.wait()
        return 0

    lax.fori_loop(0, STEPS, drain, 0)


def pitched(ref, step):
    start = step * PER * PITCH
    if not isinstance(step, int):
        start = pl.multiple_of(start, 8)
    return ref.at[pl.ds(start, PER * PITCH)]


def no_copies(i):
    return ()


def unit_mask(tall):
    return (lanes(tall) & 63) == rows_of(tall)


VMEM = pl.BlockSpec(memory_space=pltpu.VMEM)
SMEM = pl.BlockSpec(memory_space=pltpu.SMEM)
HBM = pl.BlockSpec(memory_space=pltpu.HBM)
CUBE = jax.ShapeDtypeStruct((LINES, CY, CZ), f32)
FLAT = jax.ShapeDtypeStruct((LINES, CZ), f32)
PITCHED = (LINES * PITCH, CZ)
ROWS = LINES // 2
HALO = jax.ShapeDtypeStruct((ROWS + 8, CZ), f32)


def sweep_kernel(
    u_hbm, q_hbm, eta_hbm, m_hbm, ends_ref, columns_ref, up_ref, down_ref,
    u_ref, q_ref, m_ref, x_buf, f_buf, eta_ref, eta_sem, sems,
):
    lane = lanes()
    place = ((lane + 1) >> 1) & 63

    def fetches(i):
        return (
            pltpu.make_async_copy(chunk(u_hbm, i), chunk(u_ref, i), sems.at[0, i]),
            pltpu.make_async_copy(chunk(q_hbm, i), chunk(q_ref, i), sems.at[1, i]),
        )

    def stores(i):
        return (pltpu.make_async_copy(pitched(m_ref, i), pitched(m_hbm, i), sems.at[2, i]),)

    eta_copy = pltpu.make_async_copy(eta_hbm, eta_ref, eta_sem)
    eta_copy.start()
    for i in range(AHEAD):
        for copy in fetches(i):
            copy.start()
    eta_copy.wait()
    eta = jnp.broadcast_to(eta_ref[...], (8, CZ))
    up_ref[pl.ds(ROWS, 8), :] = eta
    down_ref[pl.ds(ROWS, 8), :] = eta
    face_low = jnp.where(lane == 0, 0.0, z_rate * 0.5 * (pltpu.roll(eta, 1, 1) + eta))
    face_high = jnp.where(lane == CZ - 1, 0.0, z_rate * 0.5 * (eta + pltpu.roll(eta, CZ - 1, 1)))
    decay, peak = root_of(eta)
    groups = PER // GROUP

    size = PER * PITCH
    half = CY // 2

    def rows(i, g):
        return pl.ds(pl.multiple_of(i * PER + g * GROUP, 8), GROUP)

    def right_side(i, tiles, acc):
        for tile in tiles:
            g, k = tile // 64, tile % 64
            c, at = tile // 8, pl.ds((tile % 8) * 8, 8)
            here = u_ref[i * PER + c, at, :]
            under = pltpu.roll(here, 1, 1)
            over = pltpu.roll(here, CZ - 1, 1)
            acc = jnp.where(place == k, pltpu.roll(here, 2 * k, 1) if k else here, acc)
            q = q_ref[i * PER + c, at, :].astype(f32)
            explicit = face_high * (over - here) - face_low * (here - under)
            x_buf[pl.ds((i % 2) * size + c * PITCH + (tile % 8) * 8, 8), :] = here + explicit + q
            if k == 63:
                columns_ref[rows(i, g), :] = acc
        return acc

    def sweep(i, ahead):
        def x_at(g, y):
            return x_buf[pl.ds((i % 2) * size + g * GROUP * PITCH + y, GROUP, stride=PITCH), :]

        def at(g, y):
            return pl.ds(g * GROUP * PITCH + y, GROUP, stride=PITCH)

        def out(g, y):
            return pl.ds(i * size + g * GROUP * PITCH + y, GROUP, stride=PITCH)

        acc = jnp.zeros((8, CZ), f32)
        forth = [acc] * groups
        back = [acc] * groups
        for s in range(CY):
            low, high = s, CY - 1 - s
            for g in range(groups):
                forth[g] = forth[g] * decay + x_at(g, low)
                kept = back[g] * decay
                back[g] = kept + x_at(g, high)
                if s < half:
                    f_buf[at(g, low), :] = forth[g]
                    f_buf[at(g, high), :] = kept
                else:
                    m_ref[out(g, low), :] = peak * (forth[g] + f_buf[at(g, low), :])
                    m_ref[out(g, high), :] = peak * (f_buf[at(g, high), :] + kept)
            if ahead:
                each = PER * CY // 8 // CY
                acc = right_side(i + 1, range(s * each, (s + 1) * each), acc)
        for g in range(groups):
            ends_ref[0, rows(i, g), :] = forth[g]
            ends_ref[1, rows(i, g), :] = back[g]

    for copy in fetches(0):
        copy.wait()
    right_side(0, range(PER * CY // 8), jnp.zeros((8, CZ), f32))

    def step(i, _):
        @pl.when(i + AHEAD < STEPS)
        def _():
            for copy in fetches(i + AHEAD):
                copy.start()

        for copy in fetches(i + 1):
            copy.wait()
        sweep(i, True)
        for copy in stores(i):
            copy.start()
        return 0

    lax.fori_loop(0, STEPS - 1, step, 0)
    sweep(STEPS - 1, False)
    for copy in stores(STEPS - 1):
        copy.start()
    for i in range(STEPS):
        for copy in stores(i):
            copy.wait()
    first, second = columns_ref[:ROWS], columns_ref[ROWS:]
    odd = lanes((ROWS, CZ)) & 1 == 1
    up_ref[:ROWS] = jnp.where(odd, first, pltpu.roll(second, 1, 1))
    down_ref[:ROWS] = jnp.where(odd, pltpu.roll(second, CZ - 1, 1), first)


def sweeps(u, q, own):
    return kernel_call(
        sweep_kernel,
        [
            jax.ShapeDtypeStruct(PITCHED, f32),
            jax.ShapeDtypeStruct((2, LINES, CZ), f32),
            FLAT,
            HALO,
            HALO,
        ],
        [HBM] + [VMEM] * 4,
        [HBM] * 3,
        [
            pltpu.VMEM((LINES, CY, CZ), f32),
            pltpu.VMEM((LINES, CY, CZ), bf16),
            pltpu.VMEM(PITCHED, f32),
            pltpu.VMEM((2 * PER * PITCH, CZ), f32),
            pltpu.VMEM((PER * PITCH, CZ), f32),
            pltpu.VMEM((1, CZ), f32),
            pltpu.SemaphoreType.DMA,
            pltpu.SemaphoreType.DMA((3, STEPS)),
        ],
        name="y_sweeps",
        mib=51,
        us=12,
    )(u, q, own)


def raised(base, exponent, bits=6):
    out = jnp.ones_like(base)
    for bit in range(bits):
        out = jnp.where((exponent >> bit) & 1 == 1, out * base, out)
        base = base * base
    return out


def flux_place(l):
    return 8 * ((l >> 1) & 7) + (l >> 4), l & 1


def turned(x):
    lane, row = lanes(x.shape), rows_of(x.shape)
    for bit in range(3):
        rows, columns = 1 << bit, 16 << bit
        in_row, in_lane = (row >> bit) & 1, (lane >> (4 + bit)) & 1
        count = x.shape[0]
        forth = pltpu.roll(pltpu.roll(x, count - rows, 0), columns, 1)
        back = pltpu.roll(pltpu.roll(x, rows, 0), CZ - columns, 1)
        x = jnp.where(in_row == in_lane, x, jnp.where(in_row == 0, forth, back))
    return x


def sided_by(low):
    def sided(x):
        return jnp.where(
            low, jnp.broadcast_to(x[:, :1], low.shape), jnp.broadcast_to(x[:, CZ - 1 :], low.shape)
        )

    return sided


def line_kernel(up_ref, repair_ref, turn_ref):
    decay, _ = root_of(up_ref[pl.ds(ROWS, 8), :])
    whole = power_64(decay)
    around = whole
    for _ in range(4):
        around = around * around
    turn_ref[0] = whole
    turn_ref[1] = 1.0 / (1.0 - around)
    square = (CZ, CZ)
    y, side = flux_place(rows_of(square))
    low = side == 0
    base = sided_by(low)(decay[:1])
    place = lanes(square) == jnp.where(low, 0, CZ - 1)
    forth = jnp.where(place, raised(base, CY - 1 - y), 0.0)
    back = jnp.where(place, raised(base, y), 0.0)
    repair_ref[...] = paired(jnp.concatenate([forth, back], axis=1))


def line_matrices(up):
    shapes = [
        jax.ShapeDtypeStruct((2 * CZ, 4 * CZ), bf16),
        jax.ShapeDtypeStruct((2, 8, CZ), f32),
    ]
    return kernel_call(line_kernel, shapes, [VMEM] * 2, [VMEM], name="line_matrices")(up)


def repair_kernel(
    rank_ref, ends_ref, columns_ref, up_ref, low_ref, high_ref, repair_ref,
    out_ref, flux_ref,
):
    rank = rank_ref[0]
    inner_low, inner_high = rank > 0, rank < NGZ - 1
    own, low_eta, high_eta = (ref[pl.ds(ROWS, 8), :] for ref in (up_ref, low_ref, high_ref))
    own = own[:1]
    low_eta = jnp.where(inner_low, low_eta[:1], 0.0)[:, CZ - 1 :]
    high_eta = jnp.where(inner_high, high_eta[:1], 0.0)[:, :1]
    face_low = jnp.broadcast_to(z_rate * 0.5 * (low_eta + own[:, :1]), (1, CZ))
    face_high = jnp.broadcast_to(z_rate * 0.5 * (own[:, CZ - 1 :] + high_eta), (1, CZ))
    face = jnp.where(lanes((1, CZ)) & 1 == 0, face_low, face_high)
    face = jnp.broadcast_to(face, (ROWS, CZ))
    even = lanes((ROWS, CZ)) & 1 == 0
    low = jnp.where(inner_low, low_ref[:ROWS], 0.0)
    high = jnp.where(inner_high, high_ref[:ROWS], 0.0)
    outer = (
        jnp.where(even, pltpu.roll(low, 1, 1), pltpu.roll(high, 1, 1)),
        jnp.where(even, low, pltpu.roll(high, 2, 1)),
    )
    for half in range(2):
        at = pl.ds(half * ROWS, ROWS)
        columns = columns_ref[at, :]
        inner = jnp.where(even, columns, pltpu.roll(columns, 2, 1))
        flux = turned(face * (outer[half] - inner))
        flux_ref[at, :] = flux
        added = pair_dot(flux, repair_ref[...])
        out_ref[0, at, :] = ends_ref[0, at, :] + added[:, :CZ]
        out_ref[1, at, :] = ends_ref[1, at, :] + added[:, CZ:]


def repair(ranks, ends, columns, up, low, high, matrix):
    shapes = [
        jax.ShapeDtypeStruct((2, LINES, CZ), f32),
        FLAT,
    ]
    call = kernel_call(repair_kernel, shapes, [VMEM] * 2, [SMEM] + [VMEM] * 6, name="repair")
    return call(ranks, ends, columns, up, low, high, matrix)


def ring_kernel(
    rank_ref, ends_ref, turn_ref, near_ref, far_low_ref, far_high_ref, out_ref, eta_ref, eta_buf
):
    eta_buf[0:2, :] = far_low_ref[1:3, :]
    eta_buf[2:5, :] = near_ref[0:3, :]
    eta_buf[5:8, :] = far_high_ref[0:3, :]
    eta_ref[...] = pltpu.roll(eta_buf[...], lax.rem(rank_ref[0] + 5, 8), 0)
    rows = 2 * LINES // NGY
    upward = rank_ref[1] < NGY // 2
    whole, closing = turn_ref[0], turn_ref[1]
    for part in range(rows // 8):

        def at(node):
            return pl.ds(node * rows + part * 8, 8)

        up = jnp.zeros((8, CZ), f32)
        down = jnp.zeros((8, CZ), f32)
        for node in range(NGY):
            up = up * whole + ends_ref[at(node), :]
            down = down * whole + ends_ref[at(NGY - 1 - node), :]
        up = up * closing
        down = down * closing
        ups, downs = [], [None] * NGY
        for node in range(NGY):
            ups.append(up)
            up = up * whole + ends_ref[at(node), :]
            downs[NGY - 1 - node] = down
            down = down * whole + ends_ref[at(NGY - 1 - node), :]
        for node in range(NGY):
            out_ref[at(node), :] = jnp.where(upward, ups[node], downs[node])


def ring_scan(ranks, ends, turn, near, far_low, far_high):
    rows = jax.ShapeDtypeStruct((NGZ, CZ), f32)
    return kernel_call(
        ring_kernel,
        [jax.ShapeDtypeStruct(ends.shape, f32), rows],
        [VMEM] * 2,
        [SMEM] + [VMEM] * 5,
        [pltpu.VMEM((NGZ, CZ), f32)],
        name="ring_scan",
    )(ranks, ends, turn, near, far_low, far_high)


def coefficient_kernel(
    rank_ref, eta_ref, table_ref, green_ref, ends_ref, carry_ref, share_ref, layer_ref, reach_ref,
):
    rank = rank_ref[0]
    lane, row = lanes(), rows_of()
    eta = eta_ref[...]

    def before(x, fill):
        y = pltpu.roll(x, 1, 1)
        return jnp.where(lane == 0, jnp.where(row == 0, fill, pltpu.roll(y, 1, 0)), y)

    def after(x, fill):
        y = pltpu.roll(x, CZ - 1, 1)
        edge = jnp.where(row == NGZ - 1, fill, pltpu.roll(y, NGZ - 1, 0))
        return jnp.where(lane == CZ - 1, edge, y)

    def last_of(x, end):
        return jnp.broadcast_to(x[:, end : end + 1], (8, CZ))

    face_low = z_rate * 0.5 * (before(eta, 0.0) + eta)
    face_high = z_rate * 0.5 * (eta + after(eta, 0.0))

    def pivots(face, up):
        scale = 1.0 / (1.0 + face)
        a = jnp.ones((8, CZ), f32)
        b = face * scale
        c = scale
        d = b
        step = 1
        while step < CZ:
            shift = step if up else CZ - step
            inside = lane >= step if up else lane < CZ - step
            pa, pb, pc, pd = (pltpu.roll(x, shift, 1) for x in (a, b, c, d))
            na, nb = a * pa + b * pc, a * pb + b * pd
            nc, nd = c * pa + d * pc, c * pb + d * pd
            a, b = jnp.where(inside, na, a), jnp.where(inside, nb, b)
            c, d = jnp.where(inside, nc, c), jnp.where(inside, nd, d)
            step *= 2
        end = CZ - 1 if up else 0
        ta, tb, tc, td = (last_of(x, end) for x in (a, b, c, d))
        edge = row == (0 if up else NGZ - 1)
        va, vc = jnp.ones((8, CZ), f32), jnp.zeros((8, CZ), f32)
        for _ in range(NGZ - 1):
            na, nc = ta * va + tb * vc, tc * va + td * vc
            size = 1.0 / (na + nc)
            shift = 1 if up else NGZ - 1
            va = jnp.where(edge, 1.0, pltpu.roll(na * size, shift, 0))
            vc = jnp.where(edge, 0.0, pltpu.roll(nc * size, shift, 0))
        return (a * va + b * vc) / (c * va + d * vc)

    delta_up = pivots(face_low, True)
    delta_down = pivots(face_high, False)
    inverse = 1.0 / (delta_up + delta_down - 1.0)
    first_cell = (lane == 0) & (row == 0)
    last_cell = (lane == CZ - 1) & (row == NGZ - 1)
    link_up = jnp.where(first_cell, 0.0, face_low / (face_low + before(delta_up, 1.0)))
    link_down = jnp.where(last_cell, 0.0, face_high / (face_high + after(delta_down, 1.0)))

    def running(x, up):
        step = 1
        while step < CZ:
            moved = pltpu.roll(x, step if up else CZ - step, 1)
            x = jnp.where(lane >= step if up else lane < CZ - step, x * moved, x)
            step *= 2
        return x

    product_up, product_down = running(link_up, True), running(link_down, False)
    across_up, across_down = last_of(product_up, CZ - 1), last_of(product_down, 0)
    share_up = jnp.zeros((8, CZ), f32)
    share_down = jnp.zeros((8, CZ), f32)
    for _ in range(NGZ - 1):
        moved = pltpu.roll(across_up * share_up, NGZ - 1, 0)
        share_up = jnp.where(row == rank - 1, 1.0, jnp.where(row < rank - 1, moved, 0.0))
        moved = pltpu.roll(across_down * share_down, 1, 0)
        share_down = jnp.where(row == rank + 1, 1.0, jnp.where(row > rank + 1, moved, 0.0))

    def own(x):
        return jnp.sum(jnp.where(row == rank, x, 0.0), axis=0, keepdims=True)

    scale = own(inverse)
    own_up, own_down = own(link_up), own(link_down)
    turned_by = lax.rem(NGZ - rank, NGZ)
    share_up = share_up * jnp.broadcast_to(own_up[:, :1], (8, CZ))
    share_down = share_down * jnp.broadcast_to(own_down[:, CZ - 1 :], (8, CZ))
    share_ref[0] = pltpu.roll(share_up, turned_by, 0)
    share_ref[1] = pltpu.roll(share_down, turned_by, 0)
    lane_1 = lanes((1, CZ))
    within_up = running(jnp.broadcast_to(jnp.where(lane_1 == 0, 1.0, own_up), (8, CZ)), True)
    within_down = running(
        jnp.broadcast_to(jnp.where(lane_1 == CZ - 1, 1.0, own_down), (8, CZ)), False
    )
    square = (CZ, CZ)
    lane_sq, row_sq = lanes(square), rows_of(square)
    carry = jnp.where(
        row_sq < CZ // 2,
        jnp.broadcast_to(within_up[:1] * scale, square),
        jnp.broadcast_to(within_down[:1] * scale, square),
    )
    identity = jnp.where(lane_sq == row_sq, 1.0, 0.0).astype(f32)

    def triangle(link, up):
        link = jnp.where(lanes((1, CZ)) == (0 if up else CZ - 1), 0.0, link)
        link = jnp.broadcast_to(link, (8, CZ))
        out = identity
        step = 1
        while step < CZ:
            shift = step if up else CZ - step
            out = out + jnp.broadcast_to(link[0:1, :], square) * pltpu.roll(out, shift, 1)
            link = link * pltpu.roll(link, shift, 1)
            step *= 2
        return out

    lower, upper = triangle(own_up, True), triangle(own_down, False)
    green = 2.0 * (lower + upper - identity) * jnp.broadcast_to(scale, square)
    ends = 2.0 * jnp.where(
        lane_sq < CZ // 2,
        jnp.broadcast_to(lower[:, CZ - 1 : CZ], square),
        jnp.broadcast_to(upper[:, 0:1], square),
    )
    for matrix, ref in ((green, green_ref), (ends, ends_ref), (carry, carry_ref)):
        ref[...] = paired(matrix)

    decay, peak = root_of(own(eta))
    y = row_sq & 63
    wide = jnp.broadcast_to(decay, square)
    start = jnp.broadcast_to(peak * decay, square)
    seen = jnp.transpose(ends)
    reach = []
    for way in range(2):
        response = start * raised(wide, (y, CY - 1 - y)[way])
        table_ref[way] = response[:CY]
        reach.append(jnp.transpose(response * seen))
    reach_ref[...] = paired(jnp.concatenate(reach, axis=0))
    y, side = flux_place(row_sq)
    low = side == 0
    sided = sided_by(low)
    base = sided(decay)
    apart = jnp.abs(y - (lane_sq & 63))
    spread = jnp.where(low == (lane_sq < 64), sided(peak) * raised(base, apart), 0.0)
    same_y = (lane_sq & 63) == (row_sq & 63)
    first = jnp.broadcast_to(ends[0:1, :], square)
    final = jnp.broadcast_to(ends[CZ - 1 :, :], square)
    layer = jnp.where(same_y, jnp.where(row_sq < 64, first, final), 0.0)
    layer_ref[...] = paired(jnp.concatenate([2.0 * spread, pair_dot(spread, paired(layer))], axis=1))


def coefficients(ranks, etas):
    def matrix(rows, columns):
        return jax.ShapeDtypeStruct((2 * rows * CZ, 2 * columns * CZ), bf16)

    return kernel_call(
        coefficient_kernel,
        [
            jax.ShapeDtypeStruct((2, CY, CZ), f32),
            matrix(1, 1),
            matrix(1, 1),
            matrix(1, 1),
            jax.ShapeDtypeStruct((2, NGZ, CZ), f32),
            matrix(1, 2),
            matrix(2, 1),
        ],
        [VMEM] * 7,
        [SMEM, VMEM],
        name="z_coefficients",
        us=4,
    )(ranks, etas)


def split_rows(left_ref, rows, x):
    high, mid = split(x)
    left_ref[rows, 0:CZ] = high
    left_ref[rows, CZ : 2 * CZ] = mid


def halves(result):
    return result[:, :CZ] + result[:, CZ:]


def fetches_of(u_hbm, m_hbm, u_ref, m_ref, sems):
    def fetches(i):
        return (
            pltpu.make_async_copy(pitched(m_hbm, i), pitched(m_ref, i), sems.at[0, i]),
            pltpu.make_async_copy(chunk(u_hbm, i), chunk(u_ref, i), sems.at[1, i]),
        )

    return fetches


def sums_kernel(
    m_hbm, u_hbm, ends_ref, flux_ref, spread_ref, sums_ref, layer_ref, m_ref, u_ref, left_ref, seen_ref, sems
):
    mask = unit_mask((CY, CZ))

    def prepare():
        both = pair_dot(flux_ref[...], spread_ref[...])
        layer_ref[...] = both[:, :CZ]
        seen_ref[...] = both[:, CZ:]

    def work(i):
        near_m = pitched(m_ref, i)
        for g in range(PER // BATCH):
            left = left_ref.at[g % SLOTS]
            first = i * PER + g * BATCH
            for c in range(BATCH):
                line = first + c
                change = near_m[pl.ds((g * BATCH + c) * PITCH, CY), :] - u_ref[line]
                split_rows(left, pl.ds(c * CY, CY), change)
            result = halves(jnp.dot(left[...], ends_ref[...], preferred_element_type=f32))
            for c in range(BATCH):
                part = jnp.where(mask, result[c * CY : (c + 1) * CY], 0.0)
                sums_ref[pl.ds(first + c, 1), :] = jnp.sum(part, axis=0, keepdims=True)

    pipeline(fetches_of(u_hbm, m_hbm, u_ref, m_ref, sems), no_copies, work, prepare)
    sums_ref[...] += seen_ref[...]


def local_sums(m, u, ends, flux, spread):
    return kernel_call(
        sums_kernel,
        [FLAT, FLAT],
        [VMEM] * 2,
        [HBM, HBM] + [VMEM] * 3,
        [
            pltpu.VMEM(PITCHED, f32),
            pltpu.VMEM((LINES, CY, CZ), f32),
            pltpu.VMEM((SLOTS, BATCH * CY, 2 * CZ), bf16),
            pltpu.VMEM((LINES, CZ), f32),
            pltpu.SemaphoreType.DMA((2, STEPS)),
        ],
        name="z_local_sums",
        mib=48,
        us=8,
    )(m, u, ends, flux, spread)


def messages_kernel(rank_ref, sums_ref, carry_ref, reach_ref, *out_refs):
    rank = rank_ref[0]
    carries = jnp.concatenate([carry_ref[0], carry_ref[1]], axis=1)
    sums = sums_ref[...] + pair_dot(carries, reach_ref[...])
    first, second = sums[:ROWS], sums[ROWS:]
    lower = lanes((ROWS, CZ)) < 64
    up = jnp.where(lower, first, pltpu.roll(second, 64, 1))
    down = jnp.where(lower, pltpu.roll(first, 64, 1), second)
    for k in range(1, NGZ):
        out_refs[k - 1][...] = jnp.where(rank >= k, down, up)


def messages_of(ranks, sums, carries, reach):
    shapes = [jax.ShapeDtypeStruct((ROWS, CZ), f32)] * (NGZ - 1)
    specs = [VMEM] * (NGZ - 1)
    call = kernel_call(messages_kernel, shapes, specs, [SMEM] + [VMEM] * 3, name="z_messages")
    return call(ranks, sums, carries, reach)


def solve_kernel(
    m_hbm, u_hbm, carry_ref, table_ref, green_ref, y_ref, m_ref, u_ref, left_ref, sems
):
    tall = (CY, CZ)

    def work(i):
        near_m = pitched(m_ref, i)
        for g in range(PER // BATCH):
            left = left_ref.at[g % SLOTS]
            first = i * PER + g * BATCH
            for c in range(BATCH):
                line = first + c
                carry_up = jnp.broadcast_to(carry_ref[0, pl.ds(line, 1), :], tall)
                carry_down = jnp.broadcast_to(carry_ref[1, pl.ds(line, 1), :], tall)
                change = near_m[pl.ds((g * BATCH + c) * PITCH, CY), :] - u_ref[line]
                change = change + table_ref[0] * carry_up + table_ref[1] * carry_down
                split_rows(left, pl.ds(c * CY, CY), change)
            result = halves(jnp.dot(left[...], green_ref[...], preferred_element_type=f32))
            for c in range(BATCH):
                y_ref[first + c] = u_ref[first + c] + result[c * CY : (c + 1) * CY]

    pipeline(fetches_of(u_hbm, m_hbm, u_ref, m_ref, sems), no_copies, work)


def local_solve(m, u, carries, table, green):
    return kernel_call(
        solve_kernel,
        CUBE,
        VMEM,
        [HBM, HBM] + [VMEM] * 3,
        [
            pltpu.VMEM(PITCHED, f32),
            pltpu.VMEM((LINES, CY, CZ), f32),
            pltpu.VMEM((SLOTS, BATCH * CY, 2 * CZ), bf16),
            pltpu.SemaphoreType.DMA((3, STEPS)),
        ],
        name="z_local_solve",
        mib=42,
        us=8,
    )(m, u, carries, table, green)


def finish_kernel(
    y_ref, matrix_ref, share_ref, layer_ref, *rest
):
    got_refs = rest[: NGZ - 1]
    out_hbm, out_ref, left_ref, high_ref, mid_ref, sems = rest[NGZ - 1 :]
    lower = lanes((ROWS, CZ)) < 64
    tall = (CY, CZ)
    mask = unit_mask(tall)

    def stores(i):
        return (pltpu.make_async_copy(chunk(out_ref, i), chunk(out_hbm, i), sems.at[1, i]),)

    def prepare():
        up = jnp.zeros((ROWS, CZ), f32)
        down = jnp.zeros((ROWS, CZ), f32)
        for k in range(1, NGZ):
            value = got_refs[k - 1][...]
            up += jnp.broadcast_to(share_ref[0, k : k + 1, :], (ROWS, CZ)) * value
            down += jnp.broadcast_to(share_ref[1, k : k + 1, :], (ROWS, CZ)) * value
        both = (
            jnp.where(lower, up, pltpu.roll(down, 64, 1)),
            jnp.where(lower, pltpu.roll(up, 64, 1), down),
        )
        for half in range(2):
            at = pl.ds(half * ROWS, ROWS)
            high, mid = split(both[half] + layer_ref[at, :])
            high_ref[at, :] = high.astype(f32)
            mid_ref[at, :] = mid.astype(f32)

    def work(i):
        for g in range(PER // BATCH):
            left = left_ref.at[g % SLOTS]
            first = i * PER + g * BATCH
            for c in range(BATCH):
                line = pl.ds(first + c, 1)
                at = pl.ds(c * CY, CY)
                high = jnp.broadcast_to(high_ref[line, :], tall)
                mid = jnp.broadcast_to(mid_ref[line, :], tall)
                left[at, 0:CZ] = jnp.where(mask, high, 0.0).astype(bf16)
                left[at, CZ:] = jnp.where(mask, mid, 0.0).astype(bf16)
            result = halves(jnp.dot(left[...], matrix_ref[...], preferred_element_type=f32))
            for c in range(BATCH):
                out_ref[first + c] = y_ref[first + c] + result[c * CY : (c + 1) * CY]

    pipeline(no_copies, stores, work, prepare)


def finish(y, matrix, share, layer, got):
    return kernel_call(
        finish_kernel,
        CUBE,
        HBM,
        [VMEM] * (NGZ + 3),
        [
            pltpu.VMEM((LINES, CY, CZ), f32),
            pltpu.VMEM((SLOTS, BATCH * CY, 2 * CZ), bf16),
            pltpu.VMEM((LINES, CZ), f32),
            pltpu.VMEM((LINES, CZ), f32),
            pltpu.SemaphoreType.DMA((2, STEPS)),
        ],
        name="z_carries",
        mib=42,
        us=8,
    )(y, matrix, share, layer, *got)


def shifted(x, axis, by):
    n = lax.axis_size(axis)
    return lax.ppermute(x, axis, [(i, (i + by) % n) for i in range(n)])


def body(fields, source_term, resistivity):
    u = fields.reshape(LINES, CY, CZ)
    q = source_term.reshape(LINES, CY, CZ)
    ranks = jnp.stack([lax.axis_index("gz"), lax.axis_index("gy")]).astype(jnp.int32)
    own = resistivity.reshape(1, CZ)
    m, ends, columns, up, down = sweeps(u, q, own)
    low, high = shifted(up, "gz", 1), shifted(down, "gz", -1)
    matrix, turn = line_matrices(up)
    near = jnp.concatenate([x[ROWS : ROWS + 1] for x in (low, up, high)] + [up[ROWS + 3 :]], axis=0)
    ends, flux = repair(ranks, ends, columns, up, low, high, matrix)
    nodes = lax.all_to_all(ends.reshape(2 * LINES, CZ), "gy", 0, 0, tiled=True)
    far_low, far_high = shifted(near, "gz", 3), shifted(near, "gz", -3)
    nodes, etas = ring_scan(ranks, nodes, turn, near, far_low, far_high)
    carries = lax.all_to_all(nodes, "gy", 0, 0, tiled=True).reshape(2, LINES, CZ)
    table, green, last, vector, share, layers, reach = coefficients(ranks, etas)
    sums, layer = local_sums(m, u, last, flux, layers)
    messages = messages_of(ranks, sums, carries, reach)
    got = [shifted(x, "gz", -k) for k, x in enumerate(messages, start=1)]
    y = local_solve(m, u, carries, table, green)
    return finish(y, vector, share, layer, got).reshape(fields.shape)


def solution(mesh):
    return jax.shard_map(
        body,
        mesh=mesh,
        in_specs=(P(None, None, "gy", "gz"), P(None, None, "gy", "gz"), P("gz")),
        out_specs=P(None, None, "gy", "gz"),
        check_vma=False,
    )
```
